32 devices in a mesh: dp: 8 (over z, x), tensor: 4 (over y, core).
Axes of the slice: x: 2, y: 2, z: 4, core: 2. Of those that a mesh axis runs over, the one named last changes fastest.
Arguments:
- tokens: bfloat16 [8192, 5120], P(('dp', 'tensor')), may hold values from -6 to 6
- norm_gain: float32 [5120], replicated, may hold values from 0.1 to 1.9
- w_qkv: bfloat16 [5120, 3, 4096], P(None, None, 'tensor'), may hold values from -0.078125 to 0.078125
- qk_gain: float32 [2, 32, 128], P(None, 'tensor'), may hold values from 0.2 to 8.5
- w_out: bfloat16 [4096, 5120], P('tensor', 'dp'), may hold values from -0.5 to 0.5
- lengths: int32 [8, 4], P('dp'), may hold values from 1 to 512, 1024 in all within a row
Outputs:
- mixed: bfloat16 [8192, 5120], P(('dp', 'tensor'))
The draws below stay inside these ranges and needn't reach their ends.
Inputs may be any that keep to these rules, and one draw needn't show every extreme that they name: `lengths`: each row sums to 1024; its largest entry is exactly 512.
All inputs are finite; a program needn't handle non-finite values.
Results may differ from the reference program's by a relative error of at most 0.013.
The reference program's roundings to bfloat16 on the way count: a program that leaves them out, or rounds other values in their place, can miss the bound.
Values may be sent and summed in bfloat16 or wider, within the bound.
No kernel may reach another device: no remote copies, remote signals or barrier semaphores. Data moves between devices by JAX's collectives and lax.ppermute only.
A program may use at most 192 MiB of HBM per device.

```python
import math
import jax
import jax.numpy as jnp
import numpy as np
from jax import lax

D = 5120
HEADS = 32
HD = 128
CAP = 1024
WIN_DEV = 4
HEAD_SETS = 4
TOKENS = 8192
N_DP = 8


def draw_qk_gain(key, part):
    key = jax.random.fold_in(key, 7)
    head_key, entry_key = jax.random.split(key)
    head_scale = jnp.exp(jax.random.uniform(head_key, (2, HEADS, 1), jnp.float32, math.log(0.5), math.log(2.0)))
    entry_scale = jnp.exp(jax.random.uniform(entry_key, (2, HEADS, HD), jnp.float32, math.log(0.5), math.log(1.6)))
    return (head_scale * entry_scale).astype(jnp.float32)


def levels(key, dims, cuts, low, largest):
    def one(axis_at, parts):
        draws = jax.random.uniform(jax.random.fold_in(jax.random.fold_in(key, 6), axis_at), (parts,), jnp.float32, low / len(cuts), largest / len(cuts))
        return jnp.repeat(jnp.exp(draws), dims[axis_at] // parts).reshape((-1,) + (1,) * (len(dims) - axis_at - 1))

    gain = one(*cuts[0])
    for cut in cuts[1:]:
        gain = gain * one(*cut)
    return gain


def split_up(number_of, total, most, slope):
    loads = [(1 << 20) // math.isqrt(standing ** slope) + 1 for standing in range(2, number_of + 1)]
    surplus, given = total - most - (number_of - 1), [1] * (number_of - 1)
    while surplus > 0:
        candidates = [i for i in range(number_of - 1) if given[i] < most]
        pool, left = sum([loads[i] for i in candidates]), surplus
        for i in candidates:
            extra = min(most - given[i], max(1, left * loads[i] // pool), surplus)
            given[i] = given[i] + extra
            surplus = surplus - extra
    return np.array([most] + given)


def uneven_parts(stream_key, amount, total, bound, slope):
    if amount == 2:
        one = jax.random.randint(stream_key, (), max(1, total - bound), min(bound, total - 1) + 1)
        return jnp.stack([one, total - one])
    sizes = jnp.asarray(split_up(amount, total, bound, slope), jnp.int32)
    couples = (amount - 1) // 2
    source_of, taker = sizes[1:1 + 2 * couples:2], sizes[2:2 + 2 * couples:2]
    slack = jnp.minimum(source_of - 1, bound - taker)
    shifted = jax.random.randint(jax.random.fold_in(stream_key, 1), (couples,), 0, 1 << 20) % (slack + 1)
    sizes = sizes.at[1:1 + 2 * couples:2].set(source_of - shifted).at[2:2 + 2 * couples:2].set(taker + shifted)
    return sizes[jax.random.permutation(jax.random.fold_in(stream_key, 2), amount)]


def normal_values(key, shape, scale, most, cuts=(), kind=jnp.bfloat16):
    factor_of = levels(key, shape, cuts, -0.22, 0.18) if cuts else 1.0
    result = jax.random.normal(key, shape, jnp.float32) * scale * factor_of
    return jnp.minimum(jnp.maximum(result, -most), most).astype(kind)


def setup_inputs(seed: int = 0) -> dict:
    seeds = jax.random.split(jax.random.key(seed), 7)
    return {
        "tokens": normal_values(seeds[0], (TOKENS, D), 1.0, 6.0, ((0, 32),)),
        "norm_gain": jnp.clip(1.0 + 0.18 * jax.random.normal(seeds[1], (D,), jnp.float32), 0.1, 1.9),
        "w_qkv": normal_values(seeds[2], (D, 3, HEADS * HD), D ** -0.5, 0.078125, ((2, 4),)),
        "qk_gain": draw_qk_gain(jax.random.fold_in(seeds[6], 71), 0),
        "w_out": normal_values(seeds[4], (HEADS * HD, D), HD ** -0.5, 0.5, ((0, 4), (1, 8))),
        "lengths": jax.vmap(lambda own: uneven_parts(own, WIN_DEV, CAP, CAP // 2, 2))(jax.random.split(seeds[5], N_DP)).reshape((N_DP, WIN_DEV)).astype(jnp.int32),
    }


def unit_rms(values, epsilon):
    return values * lax.rsqrt(lax.optimization_barrier(jnp.mean(values * values, axis=-1, keepdims=True)) + epsilon)

def window_ids(window_lengths, count):
    ends = jnp.cumsum(window_lengths).astype(jnp.int32)
    places = jnp.arange(count, dtype=jnp.int32)
    segment = lax.optimization_barrier(jnp.sum((places[:, None] >= ends[None, :]).astype(jnp.int32), axis=1)).astype(jnp.int32)
    return (places, segment)

def one_group(tokens_group, window_lengths, norm_gain, flat_qkv, qk_gain, w_out):
    x_float = tokens_group.astype(jnp.float32)
    normed = (unit_rms(x_float, 1e-05) * norm_gain).astype(jnp.bfloat16)
    qkv = jnp.dot(normed, flat_qkv, preferred_element_type=jnp.float32).reshape(CAP, 3, HEADS, HD)
    queries = (unit_rms(qkv[:, 0], 1e-06) * qk_gain[0]).astype(jnp.bfloat16)
    key_rows = (unit_rms(qkv[:, 1], 1e-06) * qk_gain[1]).astype(jnp.bfloat16)
    value_rows = qkv[:, 2].astype(jnp.bfloat16)
    places, segment = window_ids(window_lengths, CAP)
    visible = (segment[:, None] == segment[None, :]) & (places[None, :] <= places[:, None])

    def one_head(index):
        query_head = lax.dynamic_index_in_dim(queries, index, 1, keepdims=False)
        key_head = lax.dynamic_index_in_dim(key_rows, index, 1, keepdims=False)
        value_head = lax.dynamic_index_in_dim(value_rows, index, 1, keepdims=False)
        scores = jnp.dot(query_head, key_head.T, preferred_element_type=jnp.float32) * HD ** (-0.5)
        scores = jnp.where(visible, scores, -jnp.inf)
        top = lax.optimization_barrier(jnp.max(scores, axis=1, keepdims=True))
        expo = jnp.exp(scores - top)
        total = lax.optimization_barrier(jnp.sum(expo, axis=1, keepdims=True))
        weights = expo.astype(jnp.bfloat16)
        summed = jnp.dot(weights, value_head, preferred_element_type=jnp.float32)
        return (summed / total).astype(jnp.bfloat16)
    heads_out = lax.map(one_head, jnp.arange(HEADS, dtype=jnp.int32))
    attended = jnp.transpose(heads_out, (1, 0, 2)).reshape(CAP, HEADS * HD)
    set_width = HEADS * HD // HEAD_SETS

    def add_part(running, index):
        offset = (index * set_width).astype(jnp.int32)
        columns = lax.dynamic_slice_in_dim(attended, offset, set_width, 1)
        weight_rows = lax.dynamic_slice_in_dim(w_out, offset, set_width, 0)
        partial_value = jnp.dot(columns, weight_rows, preferred_element_type=jnp.float32).astype(jnp.bfloat16)
        partial_value = lax.optimization_barrier(partial_value)
        return (running + partial_value.astype(jnp.float32), None)
    summed, _ = lax.scan(add_part, jnp.zeros((CAP, D), jnp.float32), jnp.arange(HEAD_SETS, dtype=jnp.int32))
    return (x_float + summed).astype(jnp.bfloat16)

def reference(tokens, norm_gain, w_qkv, qk_gain, w_out, lengths):
    flat_qkv = w_qkv.reshape(D, 3 * HEADS * HD)
    groups = tokens.reshape(N_DP, CAP, D)

    def run_group(items):
        return one_group(items[0], items[1], norm_gain, flat_qkv, qk_gain, w_out)
    mixed = lax.map(run_group, (groups, lengths))
    return mixed.reshape(TOKENS, D)
```

```python
import math

import jax
import jax.numpy as jnp
from jax import lax
from jax.experimental import pallas as pl
from jax.experimental.pallas import tpu as pltpu
from jax.sharding import PartitionSpec as P

EPS_ROW = 1e-05
EPS_HEAD = 1e-06
MIB = 1024 * 1024
BLOCK = 256
HEAD = 128
CORE, Y, LENGTHS = 0, 1, 2


def unit_rms(values, epsilon):
    return values * lax.rsqrt(jnp.mean(values * values, axis=-1, keepdims=True) + epsilon)


def qkv_kernel(groups, place_of, scalars, *refs):
    n_pieces = sum(groups)
    pieces = refs[:n_pieces]
    gain, weights, head_gain = refs[n_pieces : n_pieces + 3]
    out, normed = refs[-2], refs[-1]
    which, column = pl.program_id(0), pl.program_id(1)

    @pl.when((which == 0) & (column == 0))
    def _():
        at_piece = 0
        for index, versions in enumerate(groups):
            choice = pieces[at_piece : at_piece + versions]
            at_piece += versions
            step = 64
            start = place_of(index, scalars)

            def rows(at, carry, choice=choice, start=start):
                first = pl.multiple_of(at * step, step)
                block = choice[0][pl.ds(first, step), :].astype(jnp.float32)
                if len(choice) == 2:
                    other = choice[1][pl.ds(first, step), :].astype(jnp.float32)
                    block = jnp.where(scalars[CORE] == 0, block, other)
                block = unit_rms(block, EPS_ROW) * gain[...]
                to = pl.multiple_of(start + first, step)
                normed[pl.ds(to, step), :] = block.astype(jnp.bfloat16)
                return carry

            lax.fori_loop(0, choice[0].shape[0] // step, rows, 0)

    product = jnp.dot(normed[...], weights[0], preferred_element_type=jnp.float32)

    @pl.when(which < 2)
    def _():
        for head in range(product.shape[1] // HEAD):
            lanes = slice(head * HEAD, (head + 1) * HEAD)
            one = unit_rms(product[:, lanes], EPS_HEAD) * head_gain[0, :, lanes]
            out[0, :, lanes] = one.astype(jnp.bfloat16)

    @pl.when(which == 2)
    def _():
        out[0] = product.astype(jnp.bfloat16)


def qkv_rows(scalars, groups, place_of, row_block, gain, weights, head_gain, held, capacity):
    depth, width = weights.shape[1], weights.shape[2]
    pieces = [piece for group in groups for piece in group]
    rows = sum(group[0].shape[0] for group in groups)
    block = min(2 * BLOCK, width)
    in_specs = [pl.BlockSpec(piece.shape, lambda j, c, s: (0, 0)) for piece in pieces]
    in_specs += [
        pl.BlockSpec((1, depth), lambda j, c, s: (0, 0)),
        pl.BlockSpec((1, depth, block), lambda j, c, s: (j, 0, c)),
        pl.BlockSpec((1, 1, block), lambda j, c, s: (jnp.minimum(j, 1), 0, c)),
    ]
    operands = [scalars, *pieces, gain, weights, head_gain]
    aliases = {}
    if held is not None:
        in_specs.append(pl.BlockSpec(memory_space=pl.ANY))
        operands.append(held)
        aliases = {len(operands) - 1: 0}
    sizes = [len(group) for group in groups]
    return pl.pallas_call(
        lambda *refs: qkv_kernel(sizes, place_of, *refs),
        grid_spec=pltpu.PrefetchScalarGridSpec(
            num_scalar_prefetch=1,
            grid=(3, width // block),
            in_specs=in_specs,
            out_specs=pl.BlockSpec((1, rows, block), lambda j, c, s: (j, row_block(s), c)),
            scratch_shapes=[pltpu.VMEM((rows, depth), jnp.bfloat16)],
        ),
        out_shape=jax.ShapeDtypeStruct((3, capacity, width), jnp.bfloat16),
        input_output_aliases=aliases,
        compiler_params=pltpu.CompilerParams(vmem_limit_bytes=44 * MIB),
        cost_estimate=pl.CostEstimate(
            flops=2 * rows * depth * 3 * width,
            bytes_accessed=2 * (3 * depth * width + rows * depth + 3 * rows * width),
            transcendentals=0,
        ),
        name="qkv_rows",
    )(*operands)


def attention_kernel(first_block, n_windows, scalars, queries, keys, values, out, hidden):
    block, width = out.shape
    heads = width // HEAD
    at = first_block(scalars) + pl.program_id(0)
    first = at * block
    ends = []
    running = jnp.int32(0)
    for index in range(n_windows):
        running = running + scalars[LENGTHS + index]
        ends.append(running)
    opens = jnp.int32(0)
    for end in ends:
        opens = jnp.where(first >= end, end, opens)
    count = at - opens // block + 1
    factor = HEAD ** (-0.5) * math.log2(math.e)

    def attend(blocks):
        span = blocks * block
        start = pl.multiple_of((at - blocks + 1) * block, block)
        row = first + lax.broadcasted_iota(jnp.int32, (block, 1), 0)
        window = jnp.zeros_like(row)
        for end in ends:
            window = jnp.where(row >= end, end, window)
        column = start + lax.broadcasted_iota(jnp.int32, (block, span), 1)
        hidden[:, :span] = jnp.where((column <= row) & (column >= window), 0.0, -jnp.inf)
        for head in range(heads):
            lanes = slice(head * HEAD, (head + 1) * HEAD)
            scores = lax.dot_general(
                queries[0, :, lanes],
                keys[0, pl.ds(start, span), lanes],
                (((1,), (1,)), ((), ())),
                preferred_element_type=jnp.float32,
            )
            scores = scores + hidden[:, :span]
            top = jnp.max(scores, axis=1, keepdims=True)
            expo = jnp.exp2((scores - top) * factor)
            total = jnp.sum(expo, axis=1, keepdims=True)
            summed = jnp.dot(
                expo.astype(jnp.bfloat16),
                values[0, pl.ds(start, span), lanes],
                preferred_element_type=jnp.float32,
            )
            out[:, lanes] = (summed / total).astype(jnp.bfloat16)

    for blocks in (1, 2, 3):
        pl.when(count == blocks)(lambda blocks=blocks: attend(blocks))


def attention_rows(scalars, n_windows, qkv, first_block, n_blocks):
    _, capacity, width = qkv.shape
    return pl.pallas_call(
        lambda *refs: attention_kernel(first_block, n_windows, *refs),
        grid_spec=pltpu.PrefetchScalarGridSpec(
            num_scalar_prefetch=1,
            grid=(n_blocks,),
            in_specs=[
                pl.BlockSpec((1, BLOCK, width), lambda b, s: (0, first_block(s) + b, 0)),
                pl.BlockSpec((1, capacity, width), lambda b, s: (1, 0, 0)),
                pl.BlockSpec((1, capacity, width), lambda b, s: (2, 0, 0)),
            ],
            out_specs=pl.BlockSpec((BLOCK, width), lambda b, s: (b, 0)),
            scratch_shapes=[pltpu.VMEM((BLOCK, 3 * BLOCK), jnp.float32)],
        ),
        out_shape=jax.ShapeDtypeStruct((n_blocks * BLOCK, width), jnp.bfloat16),
        compiler_params=pltpu.CompilerParams(vmem_limit_bytes=32 * MIB),
        cost_estimate=pl.CostEstimate(
            flops=4 * n_blocks * BLOCK * 3 * BLOCK * width,
            bytes_accessed=2 * (2 * capacity * width + 2 * n_blocks * BLOCK * width),
            transcendentals=n_blocks * BLOCK * 3 * BLOCK * width // HEAD,
        ),
        name="attention_rows",
    )(scalars, qkv, qkv, qkv)


def out_kernel(n_inputs, n_shards, wanted, scalars, *refs):
    inputs, shards = refs[:n_inputs], refs[n_inputs : n_inputs + n_shards]
    outs = refs[n_inputs + n_shards : -4]
    rows_held, rows_arrived, held, arrived = refs[-4:]
    copies, at = [], 0
    for index, part in enumerate(inputs):
        to = rows_held.at[at : at + part.shape[0]]
        copies.append(pltpu.make_async_copy(part, to, rows_arrived.at[index]))
        at += part.shape[0]
    shard_copies = [
        pltpu.make_async_copy(shard, held.at[index], arrived.at[index])
        for index, shard in enumerate(shards)
    ]
    for copy in copies + shard_copies:
        copy.start()
    for copy in copies:
        copy.wait()
    rows = outs[0].shape[1]
    for index, copy in enumerate(shard_copies):
        copy.wait()
        for out, which in zip(outs, wanted, strict=True):
            place = pl.multiple_of(which(scalars[CORE]) * rows, rows)
            product = jnp.dot(
                rows_held[pl.ds(place, rows), :], held[index], preferred_element_type=jnp.float32
            )
            out[index] = product.astype(jnp.bfloat16)


def out_rows(scalars, inputs, shards, wanted):
    total = sum(part.shape[0] for part in inputs)
    depth, columns = shards[0].shape
    n, n_inputs, n_outs = len(shards), len(inputs), len(wanted)
    shape = jax.ShapeDtypeStruct((n, BLOCK, columns), jnp.bfloat16)
    whole = pl.BlockSpec(memory_space=pltpu.VMEM)
    return pl.pallas_call(
        lambda *refs: out_kernel(n_inputs, n, wanted, *refs),
        in_specs=[pl.BlockSpec(memory_space=pltpu.SMEM)]
        + [pl.BlockSpec(memory_space=pl.ANY)] * (n_inputs + n),
        out_specs=[whole] * n_outs,
        out_shape=[shape] * n_outs,
        scratch_shapes=[
            pltpu.VMEM((total, depth), jnp.bfloat16),
            pltpu.SemaphoreType.DMA((n_inputs,)),
            pltpu.VMEM((n, depth, columns), jnp.bfloat16),
            pltpu.SemaphoreType.DMA((n,)),
        ],
        compiler_params=pltpu.CompilerParams(vmem_limit_bytes=32 * MIB),
        cost_estimate=pl.CostEstimate(
            flops=2 * n_outs * BLOCK * depth * columns * n,
            bytes_accessed=2 * (total * depth + n * columns * (depth + n_outs * BLOCK)),
            transcendentals=0,
        ),
        name="out_rows",
    )(scalars, *inputs, *shards)


def final_kernel(n, cores, scalars, attended, tokens, *refs):
    terms, shards = refs[: len(cores)], refs[len(cores) : len(cores) + n]
    out, held, arrived = refs[-3:]
    step = pl.program_id(0)
    copies = [
        pltpu.make_async_copy(shard, held.at[index], arrived.at[index])
        for index, shard in enumerate(shards)
    ]

    @pl.when(step == 0)
    def _():
        for copy in copies:
            copy.start()

    for index, copy in enumerate(copies):
        pl.when(step == index)(copy.wait)
    product = jnp.dot(attended[...], held[step], preferred_element_type=jnp.float32)
    summed = product.astype(jnp.bfloat16).astype(jnp.float32)
    for term, core in zip(terms, cores, strict=True):
        value = term[0].astype(jnp.float32)
        if core is not None:
            value = jnp.where(scalars[CORE] == core, value, 0.0)
        summed = summed + value
    out[...] = (tokens[...].astype(jnp.float32) + summed).astype(jnp.bfloat16)


def final_rows(scalars, owners_at, first, attended, tokens, shards, terms, held):
    n = len(shards)
    rows = tokens.shape[0]
    depth, columns = shards[0].shape
    placed = pl.BlockSpec((rows, columns), lambda k, s: (0, s[owners_at + first + k]))
    in_specs = [pl.BlockSpec((rows, depth), lambda k, s: (s[CORE], 0)), placed]
    operands = [scalars, attended, tokens]
    for array, offset, _ in terms:
        in_specs.append(
            pl.BlockSpec((1, rows, columns), lambda k, s, offset=offset: (k + offset, 0, 0))
        )
        operands.append(array)
    in_specs += [pl.BlockSpec(memory_space=pl.ANY)] * n
    operands += shards
    aliases = {}
    if held is not None:
        in_specs.append(pl.BlockSpec(memory_space=pl.ANY))
        operands.append(held)
        aliases = {len(operands) - 1: 0}
    cores = [core for _, _, core in terms]
    return pl.pallas_call(
        lambda *refs: final_kernel(n, cores, *refs),
        grid_spec=pltpu.PrefetchScalarGridSpec(
            num_scalar_prefetch=1,
            grid=(n,),
            in_specs=in_specs,
            out_specs=placed,
            scratch_shapes=[
                pltpu.VMEM((n, depth, columns), jnp.bfloat16),
                pltpu.SemaphoreType.DMA((n,)),
            ],
        ),
        out_shape=jax.ShapeDtypeStruct(tokens.shape, jnp.bfloat16),
        input_output_aliases=aliases,
        compiler_params=pltpu.CompilerParams(vmem_limit_bytes=32 * MIB),
        cost_estimate=pl.CostEstimate(
            flops=2 * n * rows * columns * depth,
            bytes_accessed=2 * n * columns * (depth + rows * (2 + len(terms))),
            transcendentals=0,
        ),
        name="final_rows",
    )(*operands)


NEXT_Z = {0: 1, 1: 3, 3: 2, 2: 0}
BACK_Z = {after: before for before, after in NEXT_Z.items()}
RING = [(2 * z + x, 2 * NEXT_Z[z] + x) for z in range(4) for x in range(2)]
ACROSS_X = [(d, d ^ 1) for d in range(8)]
ACROSS_CORE = [(t, t ^ 1) for t in range(4)]
ACROSS_Y = [(t, t ^ 2) for t in range(4)]


def arrivals(device):
    z, x = [device // 2], device % 2
    for _ in range(3):
        z.append(BACK_Z[z[-1]])
    held_by = [(0, x), (1, x), (0, 1 - x), (2, x), (1, 1 - x), (3, x), (2, 1 - x), (3, 1 - x)]
    return [2 * z[steps] + from_x for steps, from_x in held_by]


def from_core(core):
    return [(t, t ^ 1) for t in range(4) if t % 2 == core]


def over_y(core):
    return [(t, t ^ 2) for t in range(4) if t % 2 == core]


def add_rounded(a, b):
    return (a.astype(jnp.float32) + b.astype(jnp.float32)).astype(jnp.bfloat16)


def by_links(tokens, norm_gain, w_qkv, qk_gain, w_out, lengths):
    shard_rows, depth = tokens.shape
    n_windows = lengths.shape[1]
    width = w_qkv.shape[2]
    capacity = 4 * shard_rows
    weights = jnp.transpose(w_qkv, (1, 0, 2))
    gain = norm_gain.reshape(1, depth)
    head_gain = qk_gain.reshape(2, 1, width)
    owners_at = LENGTHS + n_windows

    def ring(array):
        return lax.ppermute(array, "dp", RING)

    def across_x(array):
        return lax.ppermute(array, "dp", ACROSS_X)

    def over_tensor(array, pairs):
        return lax.ppermute(array, "tensor", pairs)

    def chip_rows(groups, place_of, row_block, held):
        return qkv_rows(
            scalars, groups, place_of, row_block, gain, weights, head_gain, held, capacity
        )

    def attend(qkv, first_block, n_blocks):
        return attention_rows(scalars, n_windows, qkv, first_block, n_blocks)

    def far_block(index):
        return lambda s: (1 - s[Y]) * 2 + index

    def first_row(index, s):
        return 0

    def of_core(core):
        return core

    def of_other(core):
        return 1 - core

    together = lax.optimization_barrier

    far_a = over_tensor(tokens, over_y(0))
    r1, x0 = ring(w_out), across_x(w_out)
    other = over_tensor(tokens, ACROSS_CORE)
    tensor = lax.axis_index("tensor")
    table = jnp.asarray([arrivals(device) for device in range(8)], jnp.int32)
    scalars = jnp.concatenate(
        [jnp.stack([tensor % 2, tensor // 2]), lengths[0], table[lax.axis_index("dp")]]
    ).astype(jnp.int32)
    qkv = chip_rows(
        [[tokens], [other]],
        lambda index, s: (s[CORE] + index - 2 * index * s[CORE]) * shard_rows,
        lambda s: s[Y],
        None,
    )
    far_a, r1, x0, qkv, tokens_b, scalars = together((far_a, r1, x0, qkv, tokens, scalars))

    far_b = over_tensor(tokens_b, over_y(1))
    r2, x1 = ring(r1), across_x(r1)
    swap_a = over_tensor(far_a, from_core(0))
    qkv = chip_rows([[far_a, swap_a]], first_row, far_block(0), qkv)
    attended_a = attend(qkv, far_block(0), 1)
    far_b, r2, x1, qkv, attended_a = together((far_b, r2, x1, qkv, attended_a))

    swap_b = over_tensor(far_b, from_core(1))
    early = [w_out, r1, x0, r2, x1]
    (part_a,) = out_rows(scalars, [attended_a], early, [lambda core: 0])
    swap_b, part_a, r2, x1 = together((swap_b, part_a, r2, x1))

    sum_a = over_tensor(part_a, ACROSS_Y)
    r3, x2 = ring(r2), across_x(r2)
    qkv = chip_rows([[swap_b, far_b]], first_row, far_block(1), qkv)
    attended_b = attend(qkv, far_block(1), 1)
    (part_b,) = out_rows(scalars, [attended_b], early, [lambda core: 0])
    r3, x2, sum_a, qkv, attended_b, part_b = together((r3, x2, sum_a, qkv, attended_b, part_b))

    arrived_b = over_tensor(part_b, from_core(0))
    sum_a_other = over_tensor(sum_a, from_core(1))
    both = [of_core, of_other]
    mine_2, theirs_2 = out_rows(scalars, [attended_a, attended_b], [r3, x2], both)
    arrived_b, sum_a_other, mine_2, theirs_2, r3, x2 = together(
        (arrived_b, sum_a_other, mine_2, theirs_2, r3, x2)
    )

    sum_b = over_tensor(add_rounded(part_b, arrived_b), over_y(1))
    half = r3.shape[0] // 2
    x3_a, x3_b = across_x(r3[:half]), ring(x2[half:])
    arrived_2 = over_tensor(theirs_2, ACROSS_CORE)
    attended_near = attend(qkv, lambda s: s[Y] * 2, 2)
    (theirs_1,) = out_rows(scalars, [attended_near], [*early, r3, x2], [of_other])
    sent_2 = add_rounded(mine_2, arrived_2)
    x3 = jnp.concatenate([x3_a, x3_b], axis=0)
    sum_b, x3, sent_2, theirs_1, attended_near = together(
        (sum_b, x3, sent_2, theirs_1, attended_near)
    )

    def final(first, shards, terms, held):
        return final_rows(
            scalars, owners_at, first, attended_near, tokens, shards, terms, held
        )

    sum_2 = over_tensor(sent_2, ACROSS_Y)
    near_1 = over_tensor(theirs_1, ACROSS_CORE)
    mine_3, theirs_3, theirs_1 = out_rows(
        scalars,
        [attended_a, attended_b, attended_near],
        [x3],
        [of_core, of_other, lambda core: 3 - core],
    )
    arrived_3 = over_tensor(theirs_3, ACROSS_CORE)
    near_2 = over_tensor(theirs_1, ACROSS_CORE)
    terms = [(near_1, 0, None), (sum_a, 0, 0), (sum_a_other, 0, 0), (sum_b, 0, 1)]
    out = final(0, early, terms, None)
    sum_2, arrived_3, near_2, mine_3, out = together((sum_2, arrived_3, near_2, mine_3, out))

    sum_3 = over_tensor(add_rounded(mine_3, arrived_3), ACROSS_Y)
    out = final(5, [r3, x2], [(near_1, 5, None), (sum_2, 0, None)], out)
    return final(7, [x3], [(near_2, 0, None), (sum_3, 0, None)], out)


def by_collectives(tokens, norm_gain, w_qkv, qk_gain, w_out, lengths):
    x_float = tokens.astype(jnp.float32)
    normed = (unit_rms(x_float, EPS_ROW) * norm_gain).astype(jnp.bfloat16)
    gathered = lax.all_gather(normed, "tensor", axis=0, tiled=True)
    full_out = lax.all_gather(w_out, "dp", axis=1, tiled=True)
    capacity = gathered.shape[0]
    _, heads, head_size = qk_gain.shape
    local_width = w_qkv.shape[2]
    qkv = jnp.dot(
        gathered, w_qkv.reshape(w_qkv.shape[0], 3 * local_width), preferred_element_type=jnp.float32
    ).reshape(capacity, 3, heads, head_size)
    queries = (unit_rms(qkv[:, 0], EPS_HEAD) * qk_gain[0]).astype(jnp.bfloat16)
    keys = (unit_rms(qkv[:, 1], EPS_HEAD) * qk_gain[1]).astype(jnp.bfloat16)
    values = qkv[:, 2].astype(jnp.bfloat16)
    ends = jnp.cumsum(lengths[0])
    places = jnp.arange(capacity, dtype=jnp.int32)
    segment = jnp.sum((places[:, None] >= ends[None, :]).astype(jnp.int32), axis=1)
    seen = (segment[:, None] == segment[None, :]) & (places[None, :] <= places[:, None])
    scores = jnp.einsum("qhd,khd->hqk", queries, keys, preferred_element_type=jnp.float32)
    scores = jnp.where(seen[None], scores * head_size ** (-0.5), -jnp.inf)
    expo = jnp.exp(scores - jnp.max(scores, axis=2, keepdims=True))
    total = jnp.sum(expo, axis=2, keepdims=True)
    summed = jnp.einsum(
        "hqk,khd->qhd", expo.astype(jnp.bfloat16), values, preferred_element_type=jnp.float32
    )
    attended = (summed / jnp.transpose(total, (1, 0, 2))).astype(jnp.bfloat16)
    partial = jnp.dot(
        attended.reshape(capacity, local_width), full_out, preferred_element_type=jnp.float32
    ).astype(jnp.bfloat16)
    reduced = lax.psum_scatter(partial, "tensor", scatter_dimension=0, tiled=True)
    return (x_float + reduced.astype(jnp.float32)).astype(jnp.bfloat16)


def solution(mesh):
    placed = (
        P(("dp", "tensor"), None),
        P(),
        P(None, None, "tensor"),
        P(None, "tensor", None),
        P("tensor", "dp"),
        P("dp", None),
    )
    known = mesh.shape["dp"] == 8 and mesh.shape["tensor"] == 4
    return jax.shard_map(
        by_links if known else by_collectives,
        mesh=mesh,
        in_specs=placed,
        out_specs=P(("dp", "tensor"), None),
        check_vma=False,
    )
```

```python
import math

import jax
import jax.numpy as jnp
from jax import lax
from jax.experimental import pallas as pl
from jax.experimental.pallas import tpu as pltpu
from jax.sharding import PartitionSpec as P

EPS_ROW = 1e-05
EPS_HEAD = 1e-06
MIB = 1024 * 1024
BLOCK = 256
HEAD = 128
CORE, Y, LENGTHS = 0, 1, 2


def unit_rms(values, epsilon):
    return values * lax.rsqrt(jnp.mean(values * values, axis=-1, keepdims=True) + epsilon)


SLOTS = 3


def weight_copies(weights, columns, held, sems):
    per = weights.shape[2] // columns

    def copy(step):
        at = pl.multiple_of(step % per * columns, columns)
        block = weights.at[step // per, :, pl.ds(at, columns)]
        return pltpu.make_async_copy(block, held.at[step % SLOTS], sems.at[step % SLOTS])

    return copy


def project(step, per, normed, copy, held, products, head_gain, out):
    def finish(product):
        which = (step - 1) // per
        for head in range(product.shape[1] // HEAD):
            lanes = slice(head * HEAD, (head + 1) * HEAD)
            value = product[:, lanes]
            one = unit_rms(value, EPS_HEAD) * head_gain[0, :, lanes]
            out[0, :, lanes] = jnp.where(which < 2, one, value).astype(jnp.bfloat16)

    @pl.when((step >= 1) & (step + SLOTS - 1 < 3 * per))
    def _():
        copy(step + SLOTS - 1).start()

    for parity in range(2):

        @pl.when((step < 3 * per) & (step % 2 == parity))
        def _(parity=parity):
            copy(step).wait()
            finish(products[1 - parity])
            products[parity][...] = jnp.dot(
                normed[...], held[step % SLOTS], preferred_element_type=jnp.float32
            )

    @pl.when(step == 3 * per)
    def _():
        finish(products[(3 * per - 1) % 2])


def near_kernel(scalars, own, other, gain, weights, head_gain, out, normed, held, sems, *products):
    step = pl.program_id(0)
    copy = weight_copies(weights, out.shape[2], held, sems)

    @pl.when(step == 0)
    def _():
        for number in range(SLOTS):
            copy(number).start()
        size = 64
        for piece, core in ((own, scalars[CORE]), (other, 1 - scalars[CORE])):

            def rows(number, carry, piece=piece, core=core):
                first = pl.multiple_of(number * size, size)
                one = piece[pl.ds(first, size), :].astype(jnp.float32)
                one = unit_rms(one, EPS_ROW) * gain[...]
                to = pl.multiple_of(core * piece.shape[0] + first, size)
                normed[pl.ds(to, size), :] = one.astype(jnp.bfloat16)
                return carry

            lax.fori_loop(0, piece.shape[0] // size, rows, 0)

    project(
        step, weights.shape[2] // out.shape[2], normed, copy, held, products, head_gain, out
    )


def finished(per):
    def at(step):
        block = jnp.clip(step - 1, 0, 3 * per - 1)
        return block // per, block % per

    return at


def near_rows(scalars, own, other, gain, weights, head_gain, capacity):
    depth, width = weights.shape[1], weights.shape[2]
    rows = own.shape[0] + other.shape[0]
    block = min(2 * BLOCK, width)
    per = width // block
    at = finished(per)
    once = pl.Buffered(1)
    return pl.pallas_call(
        near_kernel,
        grid_spec=pltpu.PrefetchScalarGridSpec(
            num_scalar_prefetch=1,
            grid=(3 * per + 1,),
            in_specs=[
                pl.BlockSpec(own.shape, lambda i, s: (0, 0), pipeline_mode=once),
                pl.BlockSpec(other.shape, lambda i, s: (0, 0), pipeline_mode=once),
                pl.BlockSpec((1, depth), lambda i, s: (0, 0)),
                pl.BlockSpec(memory_space=pl.ANY),
                pl.BlockSpec((1, 1, block), lambda i, s: (jnp.minimum(at(i)[0], 1), 0, at(i)[1])),
            ],
            out_specs=pl.BlockSpec((1, rows, block), lambda i, s: (at(i)[0], s[Y], at(i)[1])),
            scratch_shapes=[
                pltpu.VMEM((rows, depth), jnp.bfloat16),
                pltpu.VMEM((SLOTS, depth, block), jnp.bfloat16),
                pltpu.SemaphoreType.DMA((SLOTS,)),
                pltpu.VMEM((rows, block), jnp.float32),
                pltpu.VMEM((rows, block), jnp.float32),
            ],
        ),
        out_shape=jax.ShapeDtypeStruct((3, capacity, width), jnp.bfloat16),
        compiler_params=pltpu.CompilerParams(vmem_limit_bytes=48 * MIB),
        cost_estimate=pl.CostEstimate(
            flops=2 * rows * depth * 3 * width,
            bytes_accessed=2 * (3 * depth * width + rows * depth + 3 * rows * width),
            transcendentals=0,
        ),
        name="near_rows",
    )(scalars, own, other, gain, weights, head_gain)


def attend_block(scalars, n_windows, at, queries, rows_of, hidden, out):
    block, width = out.shape
    first = at * block
    ends = []
    running = jnp.int32(0)
    for index in range(n_windows):
        running = running + scalars[LENGTHS + index]
        ends.append(running)
    opens = jnp.int32(0)
    for end in ends:
        opens = jnp.where(first >= end, end, opens)
    count = at - opens // block + 1
    factor = HEAD ** (-0.5) * math.log2(math.e)

    def attend(blocks):
        span = blocks * block
        start = (at - blocks + 1) * block
        row = first + lax.broadcasted_iota(jnp.int32, (block, 1), 0)
        window = jnp.zeros_like(row)
        for end in ends:
            window = jnp.where(row >= end, end, window)
        column = start + lax.broadcasted_iota(jnp.int32, (block, span), 1)
        hidden[:, :span] = jnp.where((column <= row) & (column >= window), 0.0, -jnp.inf)
        keys, values, place = rows_of(blocks)
        for head in range(width // HEAD):
            lanes = slice(head * HEAD, (head + 1) * HEAD)
            scores = lax.dot_general(
                queries[:, lanes],
                keys[pl.ds(place, span), lanes],
                (((1,), (1,)), ((), ())),
                preferred_element_type=jnp.float32,
            )
            scores = scores + hidden[:, :span]
            top = jnp.max(scores, axis=1, keepdims=True)
            expo = jnp.exp2((scores - top) * factor)
            total = jnp.sum(expo, axis=1, keepdims=True)
            summed = jnp.dot(
                expo.astype(jnp.bfloat16),
                values[pl.ds(place, span), lanes],
                preferred_element_type=jnp.float32,
            )
            out[:, lanes] = (summed / total).astype(jnp.bfloat16)

    for blocks in (1, 2, 3):
        pl.when(count == blocks)(lambda blocks=blocks: attend(blocks))


def attention_kernel(first_block, n_windows, scalars, queries, keys, values, out, hidden):
    at = first_block(scalars) + pl.program_id(0)

    def rows_of(blocks):
        return keys.at[0], values.at[0], pl.multiple_of((at - blocks + 1) * BLOCK, BLOCK)

    attend_block(scalars, n_windows, at, queries.at[0], rows_of, hidden, out)


def attention_rows(scalars, n_windows, qkv, first_block, n_blocks):
    _, capacity, width = qkv.shape
    return pl.pallas_call(
        lambda *refs: attention_kernel(first_block, n_windows, *refs),
        grid_spec=pltpu.PrefetchScalarGridSpec(
            num_scalar_prefetch=1,
            grid=(n_blocks,),
            in_specs=[
                pl.BlockSpec((1, BLOCK, width), lambda b, s: (0, first_block(s) + b, 0)),
                pl.BlockSpec((1, capacity, width), lambda b, s: (1, 0, 0)),
                pl.BlockSpec((1, capacity, width), lambda b, s: (2, 0, 0)),
            ],
            out_specs=pl.BlockSpec((BLOCK, width), lambda b, s: (b, 0)),
            scratch_shapes=[pltpu.VMEM((BLOCK, 3 * BLOCK), jnp.float32)],
        ),
        out_shape=jax.ShapeDtypeStruct((n_blocks * BLOCK, width), jnp.bfloat16),
        compiler_params=pltpu.CompilerParams(vmem_limit_bytes=32 * MIB),
        cost_estimate=pl.CostEstimate(
            flops=4 * n_blocks * BLOCK * 3 * BLOCK * width,
            bytes_accessed=2 * (2 * capacity * width + 2 * n_blocks * BLOCK * width),
            transcendentals=n_blocks * BLOCK * 3 * BLOCK * width // HEAD,
        ),
        name="attention_rows",
    )(scalars, qkv, qkv, qkv)


def far_kernel(index, n_windows, n_shards, scalars, core0_rows, core1_rows, gain, weights, head_gain, *refs):
    qkv_held, shards = refs[0], refs[1 : 1 + n_shards]
    out_qkv, out_attended, out_partial = refs[1 + n_shards : 4 + n_shards]
    normed, queries, keys, values, hidden, held, sems, blocks, block_sems = refs[
        4 + n_shards : 13 + n_shards
    ]
    products = refs[13 + n_shards :]
    step = pl.program_id(0)
    block, width = out_attended.shape
    columns = out_qkv.shape[2]
    per = width // columns
    at = (1 - scalars[Y]) * 2 + index
    block_copy = weight_copies(weights, columns, blocks, block_sems)
    copies = [
        pltpu.make_async_copy(shard, held.at[number], sems.at[number])
        for number, shard in enumerate(shards)
    ]

    def older(back, which, to):
        rows = qkv_held.at[which, pl.ds(pl.multiple_of((at - back) * block, block), block)]
        place = to.at[(2 - back) * block : (3 - back) * block]
        return pltpu.make_async_copy(rows, place, sems.at[n_shards + 2 * back + which - 3])

    def all_older(do):
        for back in (1, 2):

            @pl.when(at >= back)
            def _(back=back):
                do(older(back, 1, keys))
                do(older(back, 2, values))

    @pl.when(step == 0)
    def _():
        for number in range(SLOTS):
            block_copy(number).start()
        all_older(lambda copy: copy.start())
        for copy in copies:
            copy.start()
        size = 64

        def rows(number, carry):
            first = pl.multiple_of(number * size, size)
            one = core0_rows[pl.ds(first, size), :].astype(jnp.float32)
            other = core1_rows[pl.ds(first, size), :].astype(jnp.float32)
            one = unit_rms(jnp.where(scalars[CORE] == 0, one, other), EPS_ROW) * gain[...]
            normed[pl.ds(first, size), :] = one.astype(jnp.bfloat16)
            return carry

        lax.fori_loop(0, block // size, rows, 0)

    project(step, per, normed, block_copy, blocks, products, head_gain, out_qkv)

    for number in range(3 * per):
        lanes = slice(number % per * columns, (number % per + 1) * columns)
        to = (queries, keys, values)[number // per]
        first = 0 if number < per else 2 * block

        @pl.when(step == number + 1)
        def _(to=to, lanes=lanes, first=first):
            to[first : first + block, lanes] = out_qkv[0]

    @pl.when(step == 3 * per)
    def _():
        all_older(lambda copy: copy.wait())
        attend_block(
            scalars, n_windows, at, queries, lambda blocks: (keys, values, (3 - blocks) * block), hidden, out_attended
        )
        for number, copy in enumerate(copies):
            copy.wait()
            product = jnp.dot(out_attended[...], held[number], preferred_element_type=jnp.float32)
            out_partial[number] = product.astype(jnp.bfloat16)


def far_rows(scalars, index, n_windows, rows, gain, weights, head_gain, qkv, shards):
    block, depth = rows[0].shape
    _, capacity, width = qkv.shape
    columns = min(2 * BLOCK, width)
    per = width // columns
    n = len(shards)
    shard_shape = shards[0].shape
    at = finished(per)
    once = pl.Buffered(1)
    whole = [pl.BlockSpec((block, depth), lambda i, s: (0, 0), pipeline_mode=once)] * 2
    somewhere = pl.BlockSpec(memory_space=pl.ANY)
    return pl.pallas_call(
        lambda *refs: far_kernel(index, n_windows, n, *refs),
        grid_spec=pltpu.PrefetchScalarGridSpec(
            num_scalar_prefetch=1,
            grid=(3 * per + 1,),
            in_specs=[
                *whole,
                pl.BlockSpec((1, depth), lambda i, s: (0, 0)),
                somewhere,
                pl.BlockSpec((1, 1, columns), lambda i, s: (jnp.minimum(at(i)[0], 1), 0, at(i)[1])),
                *[somewhere] * (1 + n),
            ],
            out_specs=[
                pl.BlockSpec(
                    (1, block, columns),
                    lambda i, s: (at(i)[0], (1 - s[Y]) * 2 + index, at(i)[1]),
                ),
                pl.BlockSpec((block, width), lambda i, s: (0, 0)),
                pl.BlockSpec((n, block, shard_shape[1]), lambda i, s: (0, 0, 0)),
            ],
            scratch_shapes=[
                pltpu.VMEM((block, depth), jnp.bfloat16),
                pltpu.VMEM((block, width), jnp.bfloat16),
                pltpu.VMEM((3 * block, width), jnp.bfloat16),
                pltpu.VMEM((3 * block, width), jnp.bfloat16),
                pltpu.VMEM((block, 3 * block), jnp.float32),
                pltpu.VMEM((n, *shard_shape), jnp.bfloat16),
                pltpu.SemaphoreType.DMA((n + 4,)),
                pltpu.VMEM((SLOTS, depth, columns), jnp.bfloat16),
                pltpu.SemaphoreType.DMA((SLOTS,)),
                pltpu.VMEM((block, columns), jnp.float32),
                pltpu.VMEM((block, columns), jnp.float32),
            ],
        ),
        out_shape=[
            jax.ShapeDtypeStruct(qkv.shape, jnp.bfloat16),
            jax.ShapeDtypeStruct((block, width), jnp.bfloat16),
            jax.ShapeDtypeStruct((n, block, shard_shape[1]), jnp.bfloat16),
        ],
        input_output_aliases={6: 0},
        compiler_params=pltpu.CompilerParams(vmem_limit_bytes=56 * MIB),
        cost_estimate=pl.CostEstimate(
            flops=2 * block * width * (3 * depth + 6 * block + n * shard_shape[1]),
            bytes_accessed=2 * (3 * depth * width + 2 * block * depth + n * shard_shape[1] * width),
            transcendentals=block * 3 * block * width // HEAD,
        ),
        name="far_rows",
    )(scalars, *rows, gain, weights, head_gain, qkv, *shards)


def out_kernel(n_inputs, n_shards, wanted, scalars, *refs):
    inputs, shards = refs[:n_inputs], refs[n_inputs : n_inputs + n_shards]
    outs = refs[n_inputs + n_shards : -4]
    rows_held, rows_arrived, held, arrived = refs[-4:]
    copies, at = [], 0
    for index, part in enumerate(inputs):
        to = rows_held.at[at : at + part.shape[0]]
        copies.append(pltpu.make_async_copy(part, to, rows_arrived.at[index]))
        at += part.shape[0]
    shard_copies = [
        pltpu.make_async_copy(shard, held.at[index], arrived.at[index])
        for index, shard in enumerate(shards)
    ]
    for copy in copies + shard_copies:
        copy.start()
    for copy in copies:
        copy.wait()
    rows = outs[0].shape[1]
    for index, copy in enumerate(shard_copies):
        copy.wait()
        for out, which in zip(outs, wanted, strict=True):
            place = pl.multiple_of(which(scalars[CORE]) * rows, rows)
            product = jnp.dot(
                rows_held[pl.ds(place, rows), :], held[index], preferred_element_type=jnp.float32
            )
            out[index] = product.astype(jnp.bfloat16)


def out_rows(scalars, inputs, shards, wanted):
    total = sum(part.shape[0] for part in inputs)
    depth, columns = shards[0].shape
    n, n_inputs, n_outs = len(shards), len(inputs), len(wanted)
    shape = jax.ShapeDtypeStruct((n, BLOCK, columns), jnp.bfloat16)
    whole = pl.BlockSpec(memory_space=pltpu.VMEM)
    return pl.pallas_call(
        lambda *refs: out_kernel(n_inputs, n, wanted, *refs),
        in_specs=[pl.BlockSpec(memory_space=pltpu.SMEM)]
        + [pl.BlockSpec(memory_space=pl.ANY)] * (n_inputs + n),
        out_specs=[whole] * n_outs,
        out_shape=[shape] * n_outs,
        scratch_shapes=[
            pltpu.VMEM((total, depth), jnp.bfloat16),
            pltpu.SemaphoreType.DMA((n_inputs,)),
            pltpu.VMEM((n, depth, columns), jnp.bfloat16),
            pltpu.SemaphoreType.DMA((n,)),
        ],
        compiler_params=pltpu.CompilerParams(vmem_limit_bytes=32 * MIB),
        cost_estimate=pl.CostEstimate(
            flops=2 * n_outs * BLOCK * depth * columns * n,
            bytes_accessed=2 * (total * depth + n * columns * (depth + n_outs * BLOCK)),
            transcendentals=0,
        ),
        name="out_rows",
    )(scalars, *inputs, *shards)


def final_kernel(n, cores, scalars, attended, tokens, *refs):
    terms, shards = refs[: len(cores)], refs[len(cores) : len(cores) + n]
    out, held, arrived = refs[-3:]
    step = pl.program_id(0)
    copies = [
        pltpu.make_async_copy(shard, held.at[index], arrived.at[index])
        for index, shard in enumerate(shards)
    ]

    @pl.when(step == 0)
    def _():
        for copy in copies:
            copy.start()

    for index, copy in enumerate(copies):
        pl.when(step == index)(copy.wait)
    product = jnp.dot(attended[...], held[step], preferred_element_type=jnp.float32)
    summed = product.astype(jnp.bfloat16).astype(jnp.float32)
    for term, core in zip(terms, cores, strict=True):
        value = term[0].astype(jnp.float32)
        if core is not None:
            value = jnp.where(scalars[CORE] == core, value, 0.0)
        summed = summed + value
    out[...] = (tokens[...].astype(jnp.float32) + summed).astype(jnp.bfloat16)


def final_rows(scalars, owners_at, first, attended, tokens, shards, terms, held):
    n = len(shards)
    rows = tokens.shape[0]
    depth, columns = shards[0].shape
    placed = pl.BlockSpec((rows, columns), lambda k, s: (0, s[owners_at + first + k]))
    in_specs = [pl.BlockSpec((rows, depth), lambda k, s: (s[CORE], 0)), placed]
    operands = [scalars, attended, tokens]
    for array, offset, _ in terms:
        in_specs.append(
            pl.BlockSpec((1, rows, columns), lambda k, s, offset=offset: (k + offset, 0, 0))
        )
        operands.append(array)
    in_specs += [pl.BlockSpec(memory_space=pl.ANY)] * n
    operands += shards
    aliases = {}
    if held is not None:
        in_specs.append(pl.BlockSpec(memory_space=pl.ANY))
        operands.append(held)
        aliases = {len(operands) - 1: 0}
    cores = [core for _, _, core in terms]
    return pl.pallas_call(
        lambda *refs: final_kernel(n, cores, *refs),
        grid_spec=pltpu.PrefetchScalarGridSpec(
            num_scalar_prefetch=1,
            grid=(n,),
            in_specs=in_specs,
            out_specs=placed,
            scratch_shapes=[
                pltpu.VMEM((n, depth, columns), jnp.bfloat16),
                pltpu.SemaphoreType.DMA((n,)),
            ],
        ),
        out_shape=jax.ShapeDtypeStruct(tokens.shape, jnp.bfloat16),
        input_output_aliases=aliases,
        compiler_params=pltpu.CompilerParams(vmem_limit_bytes=32 * MIB),
        cost_estimate=pl.CostEstimate(
            flops=2 * n * rows * columns * depth,
            bytes_accessed=2 * n * columns * (depth + rows * (2 + len(terms))),
            transcendentals=0,
        ),
        name="final_rows",
    )(*operands)


NEXT_Z = {0: 1, 1: 3, 3: 2, 2: 0}
BACK_Z = {after: before for before, after in NEXT_Z.items()}
RING = [(2 * z + x, 2 * NEXT_Z[z] + x) for z in range(4) for x in range(2)]
ACROSS_X = [(d, d ^ 1) for d in range(8)]
ACROSS_CORE = [(t, t ^ 1) for t in range(4)]
ACROSS_Y = [(t, t ^ 2) for t in range(4)]


def arrivals(device):
    z, x = [device // 2], device % 2
    for _ in range(3):
        z.append(BACK_Z[z[-1]])
    held_by = [(0, x), (1, x), (0, 1 - x), (2, x), (1, 1 - x), (3, x), (2, 1 - x), (3, 1 - x)]
    return [2 * z[steps] + from_x for steps, from_x in held_by]


def from_core(core):
    return [(t, t ^ 1) for t in range(4) if t % 2 == core]


def over_y(core):
    return [(t, t ^ 2) for t in range(4) if t % 2 == core]


def add_rounded(a, b):
    return (a.astype(jnp.float32) + b.astype(jnp.float32)).astype(jnp.bfloat16)


def by_links(tokens, norm_gain, w_qkv, qk_gain, w_out, lengths):
    shard_rows, depth = tokens.shape
    n_windows = lengths.shape[1]
    width = w_qkv.shape[2]
    capacity = 4 * shard_rows
    weights = jnp.transpose(w_qkv, (1, 0, 2))
    gain = norm_gain.reshape(1, depth)
    head_gain = qk_gain.reshape(2, 1, width)
    owners_at = LENGTHS + n_windows

    def ring(array):
        return lax.ppermute(array, "dp", RING)

    def across_x(array):
        return lax.ppermute(array, "dp", ACROSS_X)

    def over_tensor(array, pairs):
        return lax.ppermute(array, "tensor", pairs)

    def far(index, rows, qkv, shards):
        return far_rows(
            scalars, index, n_windows, rows, gain, weights, head_gain, qkv, shards
        )

    def of_core(core):
        return core

    def of_other(core):
        return 1 - core

    together = lax.optimization_barrier

    far_a = over_tensor(tokens, over_y(0))
    r1, x0 = ring(w_out), across_x(w_out)
    other = over_tensor(tokens, ACROSS_CORE)
    tensor = lax.axis_index("tensor")
    table = jnp.asarray([arrivals(device) for device in range(8)], jnp.int32)
    scalars = jnp.concatenate(
        [jnp.stack([tensor % 2, tensor // 2]), lengths[0], table[lax.axis_index("dp")]]
    ).astype(jnp.int32)
    qkv = near_rows(scalars, tokens, other, gain, weights, head_gain, capacity)
    far_a, r1, x0, qkv, tokens_b, scalars = together((far_a, r1, x0, qkv, tokens, scalars))

    far_b = over_tensor(tokens_b, over_y(1))
    r2, x1 = ring(r1), across_x(r1)
    swap_a = over_tensor(far_a, from_core(0))
    qkv, attended_a, part_a1 = far(0, [far_a, swap_a], qkv, [w_out, r1, x0])
    sent_a1 = add_rounded(part_a1, over_tensor(part_a1, from_core(1)))
    far_b, r2, x1, qkv, attended_a, sent_a1 = together((far_b, r2, x1, qkv, attended_a, sent_a1))

    swap_b = over_tensor(far_b, from_core(1))
    (part_a2,) = out_rows(scalars, [attended_a], [r2, x1], [lambda core: 0])
    r3, x2 = ring(r2), across_x(r2)
    sum_a1 = over_tensor(sent_a1, over_y(0))
    sum_a2 = over_tensor(part_a2, ACROSS_Y)
    early = [w_out, r1, x0, r2, x1]
    qkv, attended_b, part_b = far(1, [swap_b, far_b], qkv, early)
    r3, x2, sum_a1, sum_a2, qkv, attended_b, part_b = together(
        (r3, x2, sum_a1, sum_a2, qkv, attended_b, part_b)
    )

    arrived_b = over_tensor(part_b, from_core(0))
    both = [of_core, of_other]
    mine_2, theirs_2 = out_rows(scalars, [attended_a, attended_b], [r3, x2], both)
    arrived_b, mine_2, theirs_2, r3, x2 = together((arrived_b, mine_2, theirs_2, r3, x2))

    sum_b = over_tensor(add_rounded(part_b, arrived_b), over_y(1))
    half = r3.shape[0] // 2
    x3_a, x3_b = across_x(r3[:half]), ring(x2[half:])
    arrived_2 = over_tensor(theirs_2, ACROSS_CORE)
    sum_a2_other = over_tensor(sum_a2, from_core(1))
    attended_near = attention_rows(scalars, n_windows, qkv, lambda s: s[Y] * 2, 2)
    (theirs_1,) = out_rows(scalars, [attended_near], [*early, r3, x2], [of_other])
    sent_2 = add_rounded(mine_2, arrived_2)
    x3 = jnp.concatenate([x3_a, x3_b], axis=0)
    sum_b, x3, sent_2, theirs_1, attended_near, sum_a2_other = together(
        (sum_b, x3, sent_2, theirs_1, attended_near, sum_a2_other)
    )

    def final(first, shards, terms, held):
        return final_rows(
            scalars, owners_at, first, attended_near, tokens, shards, terms, held
        )

    sum_2 = over_tensor(sent_2, ACROSS_Y)
    near_1 = over_tensor(theirs_1, ACROSS_CORE)
    mine_3, theirs_3, theirs_1 = out_rows(
        scalars,
        [attended_a, attended_b, attended_near],
        [x3],
        [of_core, of_other, lambda core: 3 - core],
    )
    arrived_3 = over_tensor(theirs_3, ACROSS_CORE)
    near_2 = over_tensor(theirs_1, ACROSS_CORE)
    out = final(0, early[:3], [(near_1, 0, None), (sum_a1, 0, 0), (sum_b, 0, 1)], None)
    terms = [(near_1, 3, None), (sum_a2, 0, 0), (sum_a2_other, 0, 0), (sum_b, 3, 1)]
    out = final(3, early[3:], terms, out)
    sum_2, arrived_3, near_2, mine_3, out = together((sum_2, arrived_3, near_2, mine_3, out))

    sum_3 = over_tensor(add_rounded(mine_3, arrived_3), ACROSS_Y)
    out = final(5, [r3, x2], [(near_1, 5, None), (sum_2, 0, None)], out)
    return final(7, [x3], [(near_2, 0, None), (sum_3, 0, None)], out)


def by_collectives(tokens, norm_gain, w_qkv, qk_gain, w_out, lengths):
    x_float = tokens.astype(jnp.float32)
    normed = (unit_rms(x_float, EPS_ROW) * norm_gain).astype(jnp.bfloat16)
    gathered = lax.all_gather(normed, "tensor", axis=0, tiled=True)
    full_out = lax.all_gather(w_out, "dp", axis=1, tiled=True)
    capacity = gathered.shape[0]
    _, heads, head_size = qk_gain.shape
    local_width = w_qkv.shape[2]
    qkv = jnp.dot(
        gathered, w_qkv.reshape(w_qkv.shape[0], 3 * local_width), preferred_element_type=jnp.float32
    ).reshape(capacity, 3, heads, head_size)
    queries = (unit_rms(qkv[:, 0], EPS_HEAD) * qk_gain[0]).astype(jnp.bfloat16)
    keys = (unit_rms(qkv[:, 1], EPS_HEAD) * qk_gain[1]).astype(jnp.bfloat16)
    values = qkv[:, 2].astype(jnp.bfloat16)
    ends = jnp.cumsum(lengths[0])
    places = jnp.arange(capacity, dtype=jnp.int32)
    segment = jnp.sum((places[:, None] >= ends[None, :]).astype(jnp.int32), axis=1)
    seen = (segment[:, None] == segment[None, :]) & (places[None, :] <= places[:, None])
    scores = jnp.einsum("qhd,khd->hqk", queries, keys, preferred_element_type=jnp.float32)
    scores = jnp.where(seen[None], scores * head_size ** (-0.5), -jnp.inf)
    expo = jnp.exp(scores - jnp.max(scores, axis=2, keepdims=True))
    total = jnp.sum(expo, axis=2, keepdims=True)
    summed = jnp.einsum(
        "hqk,khd->qhd", expo.astype(jnp.bfloat16), values, preferred_element_type=jnp.float32
    )
    attended = (summed / jnp.transpose(total, (1, 0, 2))).astype(jnp.bfloat16)
    partial = jnp.dot(
        attended.reshape(capacity, local_width), full_out, preferred_element_type=jnp.float32
    ).astype(jnp.bfloat16)
    reduced = lax.psum_scatter(partial, "tensor", scatter_dimension=0, tiled=True)
    return (x_float + reduced.astype(jnp.float32)).astype(jnp.bfloat16)


def solution(mesh):
    placed = (
        P(("dp", "tensor"), None),
        P(),
        P(None, None, "tensor"),
        P(None, "tensor", None),
        P("tensor", "dp"),
        P("dp", None),
    )
    known = mesh.shape["dp"] == 8 and mesh.shape["tensor"] == 4
    return jax.shard_map(
        by_links if known else by_collectives,
        mesh=mesh,
        in_specs=placed,
        out_specs=P(("dp", "tensor"), None),
        check_vma=False,
    )
```

```python
import math

import jax
import jax.numpy as jnp
from jax import lax
from jax.experimental import pallas as pl
from jax.experimental.pallas import tpu as pltpu
from jax.sharding import PartitionSpec as P

EPS_ROW = 1e-05
EPS_HEAD = 1e-06
MIB = 1024 * 1024
BLOCK = 256
HEAD = 128
CORE, Y, LENGTHS = 0, 1, 2


def unit_rms(values, epsilon):
    return values * lax.rsqrt(jnp.mean(values * values, axis=-1, keepdims=True) + epsilon)


SLOTS = 3


def weight_copies(weights, columns, held, sems):
    per = weights.shape[2] // columns

    def copy(step):
        at = pl.multiple_of(step % per * columns, columns)
        block = weights.at[step // per, :, pl.ds(at, columns)]
        return pltpu.make_async_copy(block, held.at[step % SLOTS], sems.at[step % SLOTS])

    return copy


def project(step, per, normed, copy, held, products, head_gain, out):
    def finish(product):
        which = (step - 1) // per
        for head in range(product.shape[1] // HEAD):
            lanes = slice(head * HEAD, (head + 1) * HEAD)
            value = product[:, lanes]
            one = unit_rms(value, EPS_HEAD) * head_gain[0, :, lanes]
            out[0, :, lanes] = jnp.where(which < 2, one, value).astype(jnp.bfloat16)

    @pl.when((step >= 1) & (step + SLOTS - 1 < 3 * per))
    def _():
        copy(step + SLOTS - 1).start()

    for parity in range(2):

        @pl.when((step < 3 * per) & (step % 2 == parity))
        def _(parity=parity):
            copy(step).wait()
            finish(products[1 - parity])
            products[parity][...] = jnp.dot(
                normed[...], held[step % SLOTS], preferred_element_type=jnp.float32
            )

    @pl.when(step == 3 * per)
    def _():
        finish(products[(3 * per - 1) % 2])


def near_kernel(scalars, own, other, gain, weights, head_gain, out, normed, held, sems, *products):
    step = pl.program_id(0)
    copy = weight_copies(weights, out.shape[2], held, sems)

    @pl.when(step == 0)
    def _():
        for number in range(SLOTS):
            copy(number).start()
        size = 64
        for piece, core in ((own, scalars[CORE]), (other, 1 - scalars[CORE])):

            def rows(number, carry, piece=piece, core=core):
                first = pl.multiple_of(number * size, size)
                one = piece[pl.ds(first, size), :].astype(jnp.float32)
                one = unit_rms(one, EPS_ROW) * gain[...]
                to = pl.multiple_of(core * piece.shape[0] + first, size)
                normed[pl.ds(to, size), :] = one.astype(jnp.bfloat16)
                return carry

            lax.fori_loop(0, piece.shape[0] // size, rows, 0)

    project(
        step, weights.shape[2] // out.shape[2], normed, copy, held, products, head_gain, out
    )


def finished(per):
    def at(step):
        block = jnp.clip(step - 1, 0, 3 * per - 1)
        return block // per, block % per

    return at


def near_rows(scalars, own, other, gain, weights, head_gain, capacity):
    depth, width = weights.shape[1], weights.shape[2]
    rows = own.shape[0] + other.shape[0]
    block = min(2 * BLOCK, width)
    per = width // block
    at = finished(per)
    once = pl.Buffered(1)
    return pl.pallas_call(
        near_kernel,
        grid_spec=pltpu.PrefetchScalarGridSpec(
            num_scalar_prefetch=1,
            grid=(3 * per + 1,),
            in_specs=[
                pl.BlockSpec(own.shape, lambda i, s: (0, 0), pipeline_mode=once),
                pl.BlockSpec(other.shape, lambda i, s: (0, 0), pipeline_mode=once),
                pl.BlockSpec((1, depth), lambda i, s: (0, 0)),
                pl.BlockSpec(memory_space=pl.ANY),
                pl.BlockSpec((1, 1, block), lambda i, s: (jnp.minimum(at(i)[0], 1), 0, at(i)[1])),
            ],
            out_specs=pl.BlockSpec((1, rows, block), lambda i, s: (at(i)[0], s[Y], at(i)[1])),
            scratch_shapes=[
                pltpu.VMEM((rows, depth), jnp.bfloat16),
                pltpu.VMEM((SLOTS, depth, block), jnp.bfloat16),
                pltpu.SemaphoreType.DMA((SLOTS,)),
                pltpu.VMEM((rows, block), jnp.float32),
                pltpu.VMEM((rows, block), jnp.float32),
            ],
        ),
        out_shape=jax.ShapeDtypeStruct((3, capacity, width), jnp.bfloat16),
        compiler_params=pltpu.CompilerParams(vmem_limit_bytes=48 * MIB),
        cost_estimate=pl.CostEstimate(
            flops=2 * rows * depth * 3 * width,
            bytes_accessed=2 * (3 * depth * width + rows * depth + 3 * rows * width),
            transcendentals=0,
        ),
        name="near_rows",
    )(scalars, own, other, gain, weights, head_gain)


def attend_block(scalars, n_windows, at, queries, rows_of, hidden, out):
    block, width = out.shape
    first = at * block
    ends = []
    running = jnp.int32(0)
    for index in range(n_windows):
        running = running + scalars[LENGTHS + index]
        ends.append(running)
    opens = jnp.int32(0)
    for end in ends:
        opens = jnp.where(first >= end, end, opens)
    count = at - opens // block + 1
    factor = HEAD ** (-0.5) * math.log2(math.e)

    def attend(blocks):
        span = blocks * block
        start = (at - blocks + 1) * block
        row = first + lax.broadcasted_iota(jnp.int32, (block, 1), 0)
        window = jnp.zeros_like(row)
        for end in ends:
            window = jnp.where(row >= end, end, window)
        column = start + lax.broadcasted_iota(jnp.int32, (block, span), 1)
        hidden[:, :span] = jnp.where((column <= row) & (column >= window), 0.0, -jnp.inf)
        keys, values, place = rows_of(blocks)
        for head in range(width // HEAD):
            lanes = slice(head * HEAD, (head + 1) * HEAD)
            scores = lax.dot_general(
                queries[:, lanes],
                keys[pl.ds(place, span), lanes],
                (((1,), (1,)), ((), ())),
                preferred_element_type=jnp.float32,
            )
            scores = scores + hidden[:, :span]
            top = jnp.max(scores, axis=1, keepdims=True)
            expo = jnp.exp2((scores - top) * factor)
            total = jnp.sum(expo, axis=1, keepdims=True)
            summed = jnp.dot(
                expo.astype(jnp.bfloat16),
                values[pl.ds(place, span), lanes],
                preferred_element_type=jnp.float32,
            )
            out[:, lanes] = (summed / total).astype(jnp.bfloat16)

    for blocks in (1, 2, 3):
        pl.when(count == blocks)(lambda blocks=blocks: attend(blocks))


def attention_kernel(first_block, n_windows, scalars, queries, keys, values, out, hidden):
    at = first_block(scalars) + pl.program_id(0)

    def rows_of(blocks):
        return keys.at[0], values.at[0], pl.multiple_of((at - blocks + 1) * BLOCK, BLOCK)

    attend_block(scalars, n_windows, at, queries.at[0], rows_of, hidden, out)


def attention_rows(scalars, n_windows, qkv, first_block, n_blocks):
    _, capacity, width = qkv.shape
    return pl.pallas_call(
        lambda *refs: attention_kernel(first_block, n_windows, *refs),
        grid_spec=pltpu.PrefetchScalarGridSpec(
            num_scalar_prefetch=1,
            grid=(n_blocks,),
            in_specs=[
                pl.BlockSpec((1, BLOCK, width), lambda b, s: (0, first_block(s) + b, 0)),
                pl.BlockSpec((1, capacity, width), lambda b, s: (1, 0, 0)),
                pl.BlockSpec((1, capacity, width), lambda b, s: (2, 0, 0)),
            ],
            out_specs=pl.BlockSpec((BLOCK, width), lambda b, s: (b, 0)),
            scratch_shapes=[pltpu.VMEM((BLOCK, 3 * BLOCK), jnp.float32)],
        ),
        out_shape=jax.ShapeDtypeStruct((n_blocks * BLOCK, width), jnp.bfloat16),
        compiler_params=pltpu.CompilerParams(vmem_limit_bytes=32 * MIB),
        cost_estimate=pl.CostEstimate(
            flops=4 * n_blocks * BLOCK * 3 * BLOCK * width,
            bytes_accessed=2 * (2 * capacity * width + 2 * n_blocks * BLOCK * width),
            transcendentals=n_blocks * BLOCK * 3 * BLOCK * width // HEAD,
        ),
        name="attention_rows",
    )(scalars, qkv, qkv, qkv)


def far_kernel(index, n_windows, n_shards, scalars, core0_rows, core1_rows, gain, weights, head_gain, *refs):
    qkv_held, shards = refs[0], refs[1 : 1 + n_shards]
    out_qkv, out_attended, out_partial = refs[1 + n_shards : 4 + n_shards]
    normed, queries, keys, values, hidden, held, sems, blocks, block_sems = refs[
        4 + n_shards : 13 + n_shards
    ]
    products = refs[13 + n_shards :]
    step = pl.program_id(0)
    block, width = out_attended.shape
    columns = out_qkv.shape[2]
    per = width // columns
    at = (1 - scalars[Y]) * 2 + index
    block_copy = weight_copies(weights, columns, blocks, block_sems)
    copies = [
        pltpu.make_async_copy(shard, held.at[number], sems.at[number])
        for number, shard in enumerate(shards)
    ]

    def older(back, which, to):
        rows = qkv_held.at[which, pl.ds(pl.multiple_of((at - back) * block, block), block)]
        place = to.at[(2 - back) * block : (3 - back) * block]
        return pltpu.make_async_copy(rows, place, sems.at[n_shards + 2 * back + which - 3])

    def all_older(do):
        for back in (1, 2):

            @pl.when(at >= back)
            def _(back=back):
                do(older(back, 1, keys))
                do(older(back, 2, values))

    @pl.when(step == 0)
    def _():
        for number in range(SLOTS):
            block_copy(number).start()
        all_older(lambda copy: copy.start())
        for copy in copies:
            copy.start()
        size = 64

        def rows(number, carry):
            first = pl.multiple_of(number * size, size)
            one = core0_rows[pl.ds(first, size), :].astype(jnp.float32)
            other = core1_rows[pl.ds(first, size), :].astype(jnp.float32)
            one = unit_rms(jnp.where(scalars[CORE] == 0, one, other), EPS_ROW) * gain[...]
            normed[pl.ds(first, size), :] = one.astype(jnp.bfloat16)
            return carry

        lax.fori_loop(0, block // size, rows, 0)

    project(step, per, normed, block_copy, blocks, products, head_gain, out_qkv)

    for number in range(3 * per):
        lanes = slice(number % per * columns, (number % per + 1) * columns)
        to = (queries, keys, values)[number // per]
        first = 0 if number < per else 2 * block

        @pl.when(step == number + 1)
        def _(to=to, lanes=lanes, first=first):
            to[first : first + block, lanes] = out_qkv[0]

    @pl.when(step == 3 * per)
    def _():
        all_older(lambda copy: copy.wait())
        attend_block(
            scalars, n_windows, at, queries, lambda blocks: (keys, values, (3 - blocks) * block), hidden, out_attended
        )
        for number, copy in enumerate(copies):
            copy.wait()
            product = jnp.dot(out_attended[...], held[number], preferred_element_type=jnp.float32)
            out_partial[number] = product.astype(jnp.bfloat16)


def far_rows(scalars, index, n_windows, rows, gain, weights, head_gain, qkv, shards):
    block, depth = rows[0].shape
    _, capacity, width = qkv.shape
    columns = min(2 * BLOCK, width)
    per = width // columns
    n = len(shards)
    shard_shape = shards[0].shape
    at = finished(per)
    once = pl.Buffered(1)
    whole = [pl.BlockSpec((block, depth), lambda i, s: (0, 0), pipeline_mode=once)] * 2
    somewhere = pl.BlockSpec(memory_space=pl.ANY)
    return pl.pallas_call(
        lambda *refs: far_kernel(index, n_windows, n, *refs),
        grid_spec=pltpu.PrefetchScalarGridSpec(
            num_scalar_prefetch=1,
            grid=(3 * per + 1,),
            in_specs=[
                *whole,
                pl.BlockSpec((1, depth), lambda i, s: (0, 0)),
                somewhere,
                pl.BlockSpec((1, 1, columns), lambda i, s: (jnp.minimum(at(i)[0], 1), 0, at(i)[1])),
                *[somewhere] * (1 + n),
            ],
            out_specs=[
                pl.BlockSpec(
                    (1, block, columns),
                    lambda i, s: (at(i)[0], (1 - s[Y]) * 2 + index, at(i)[1]),
                ),
                pl.BlockSpec((block, width), lambda i, s: (0, 0)),
                pl.BlockSpec((n, block, shard_shape[1]), lambda i, s: (0, 0, 0)),
            ],
            scratch_shapes=[
                pltpu.VMEM((block, depth), jnp.bfloat16),
                pltpu.VMEM((block, width), jnp.bfloat16),
                pltpu.VMEM((3 * block, width), jnp.bfloat16),
                pltpu.VMEM((3 * block, width), jnp.bfloat16),
                pltpu.VMEM((block, 3 * block), jnp.float32),
                pltpu.VMEM((n, *shard_shape), jnp.bfloat16),
                pltpu.SemaphoreType.DMA((n + 4,)),
                pltpu.VMEM((SLOTS, depth, columns), jnp.bfloat16),
                pltpu.SemaphoreType.DMA((SLOTS,)),
                pltpu.VMEM((block, columns), jnp.float32),
                pltpu.VMEM((block, columns), jnp.float32),
            ],
        ),
        out_shape=[
            jax.ShapeDtypeStruct(qkv.shape, jnp.bfloat16),
            jax.ShapeDtypeStruct((block, width), jnp.bfloat16),
            jax.ShapeDtypeStruct((n, block, shard_shape[1]), jnp.bfloat16),
        ],
        input_output_aliases={6: 0},
        compiler_params=pltpu.CompilerParams(vmem_limit_bytes=56 * MIB),
        cost_estimate=pl.CostEstimate(
            flops=2 * block * width * (3 * depth + 6 * block + n * shard_shape[1]),
            bytes_accessed=2 * (3 * depth * width + 2 * block * depth + n * shard_shape[1] * width),
            transcendentals=block * 3 * block * width // HEAD,
        ),
        name="far_rows",
    )(scalars, *rows, gain, weights, head_gain, qkv, *shards)


def out_kernel(n_inputs, n_shards, wanted, scalars, *refs):
    inputs, shards = refs[:n_inputs], refs[n_inputs : n_inputs + n_shards]
    outs = refs[n_inputs + n_shards : -4]
    rows_held, rows_arrived, held, arrived = refs[-4:]
    copies, at = [], 0
    for index, part in enumerate(inputs):
        to = rows_held.at[at : at + part.shape[0]]
        copies.append(pltpu.make_async_copy(part, to, rows_arrived.at[index]))
        at += part.shape[0]
    shard_copies = [
        pltpu.make_async_copy(shard, held.at[index], arrived.at[index])
        for index, shard in enumerate(shards)
    ]
    for copy in copies + shard_copies:
        copy.start()
    for copy in copies:
        copy.wait()
    rows = outs[0].shape[1]
    for index, copy in enumerate(shard_copies):
        copy.wait()
        for out, which in zip(outs, wanted, strict=True):
            place = pl.multiple_of(which(scalars[CORE]) * rows, rows)
            product = jnp.dot(
                rows_held[pl.ds(place, rows), :], held[index], preferred_element_type=jnp.float32
            )
            out[index] = product.astype(jnp.bfloat16)


def out_rows(scalars, inputs, shards, wanted):
    total = sum(part.shape[0] for part in inputs)
    depth, columns = shards[0].shape
    n, n_inputs, n_outs = len(shards), len(inputs), len(wanted)
    shape = jax.ShapeDtypeStruct((n, BLOCK, columns), jnp.bfloat16)
    whole = pl.BlockSpec(memory_space=pltpu.VMEM)
    return pl.pallas_call(
        lambda *refs: out_kernel(n_inputs, n, wanted, *refs),
        in_specs=[pl.BlockSpec(memory_space=pltpu.SMEM)]
        + [pl.BlockSpec(memory_space=pl.ANY)] * (n_inputs + n),
        out_specs=[whole] * n_outs,
        out_shape=[shape] * n_outs,
        scratch_shapes=[
            pltpu.VMEM((total, depth), jnp.bfloat16),
            pltpu.SemaphoreType.DMA((n_inputs,)),
            pltpu.VMEM((n, depth, columns), jnp.bfloat16),
            pltpu.SemaphoreType.DMA((n,)),
        ],
        compiler_params=pltpu.CompilerParams(vmem_limit_bytes=32 * MIB),
        cost_estimate=pl.CostEstimate(
            flops=2 * n_outs * BLOCK * depth * columns * n,
            bytes_accessed=2 * (total * depth + n * columns * (depth + n_outs * BLOCK)),
            transcendentals=0,
        ),
        name="out_rows",
    )(scalars, *inputs, *shards)


def final_kernel(n, cores, scalars, attended, tokens, *refs):
    terms, shards = refs[: len(cores)], refs[len(cores) : len(cores) + n]
    out, held, arrived = refs[-3:]
    step = pl.program_id(0)
    copies = [
        pltpu.make_async_copy(shard, held.at[index], arrived.at[index])
        for index, shard in enumerate(shards)
    ]

    @pl.when(step == 0)
    def _():
        for copy in copies:
            copy.start()

    for index, copy in enumerate(copies):
        pl.when(step == index)(copy.wait)
    product = jnp.dot(attended[...], held[step], preferred_element_type=jnp.float32)
    summed = product.astype(jnp.bfloat16).astype(jnp.float32)
    for term, core in zip(terms, cores, strict=True):
        value = term[0].astype(jnp.float32)
        if core is not None:
            value = jnp.where(scalars[CORE] == core, value, 0.0)
        summed = summed + value
    out[...] = (tokens[...].astype(jnp.float32) + summed).astype(jnp.bfloat16)


def final_rows(scalars, owners_at, first, attended, tokens, shards, terms, held):
    n = len(shards)
    rows = tokens.shape[0]
    depth, columns = shards[0].shape
    placed = pl.BlockSpec((rows, columns), lambda k, s: (0, s[owners_at + first + k]))
    in_specs = [pl.BlockSpec((rows, depth), lambda k, s: (s[CORE], 0)), placed]
    operands = [scalars, attended, tokens]
    for array, offset, _ in terms:
        in_specs.append(
            pl.BlockSpec((1, rows, columns), lambda k, s, offset=offset: (k + offset, 0, 0))
        )
        operands.append(array)
    in_specs += [pl.BlockSpec(memory_space=pl.ANY)] * n
    operands += shards
    aliases = {}
    if held is not None:
        in_specs.append(pl.BlockSpec(memory_space=pl.ANY))
        operands.append(held)
        aliases = {len(operands) - 1: 0}
    cores = [core for _, _, core in terms]
    return pl.pallas_call(
        lambda *refs: final_kernel(n, cores, *refs),
        grid_spec=pltpu.PrefetchScalarGridSpec(
            num_scalar_prefetch=1,
            grid=(n,),
            in_specs=in_specs,
            out_specs=placed,
            scratch_shapes=[
                pltpu.VMEM((n, depth, columns), jnp.bfloat16),
                pltpu.SemaphoreType.DMA((n,)),
            ],
        ),
        out_shape=jax.ShapeDtypeStruct(tokens.shape, jnp.bfloat16),
        input_output_aliases=aliases,
        compiler_params=pltpu.CompilerParams(vmem_limit_bytes=32 * MIB),
        cost_estimate=pl.CostEstimate(
            flops=2 * n * rows * columns * depth,
            bytes_accessed=2 * n * columns * (depth + rows * (2 + len(terms))),
            transcendentals=0,
        ),
        name="final_rows",
    )(*operands)


NEXT_Z = {0: 1, 1: 3, 3: 2, 2: 0}
BACK_Z = {after: before for before, after in NEXT_Z.items()}
RING = [(2 * z + x, 2 * NEXT_Z[z] + x) for z in range(4) for x in range(2)]
ACROSS_X = [(d, d ^ 1) for d in range(8)]
ACROSS_CORE = [(t, t ^ 1) for t in range(4)]
ACROSS_Y = [(t, t ^ 2) for t in range(4)]


def arrivals(device):
    z, x = [device // 2], device % 2
    for _ in range(3):
        z.append(BACK_Z[z[-1]])
    held_by = [(0, x), (1, x), (0, 1 - x), (2, x), (1, 1 - x), (3, x), (2, 1 - x), (3, 1 - x)]
    return [2 * z[steps] + from_x for steps, from_x in held_by]


def from_core(core):
    return [(t, t ^ 1) for t in range(4) if t % 2 == core]


def over_y(core):
    return [(t, t ^ 2) for t in range(4) if t % 2 == core]


def ahead_kernel(scalars, attended, tokens, shard, term, out):
    product = jnp.dot(attended[...], shard[...], preferred_element_type=jnp.float32)
    summed = product.astype(jnp.bfloat16).astype(jnp.float32) + term[0].astype(jnp.float32)
    out[...] = tokens[...].astype(jnp.float32) + summed


def sum_ahead(scalars, owner_at, attended, tokens, shard, term):
    rows = tokens.shape[0]
    depth, columns = shard.shape
    return pl.pallas_call(
        ahead_kernel,
        grid_spec=pltpu.PrefetchScalarGridSpec(
            num_scalar_prefetch=1,
            grid=(1,),
            in_specs=[
                pl.BlockSpec((rows, depth), lambda k, s: (s[CORE], 0)),
                pl.BlockSpec((rows, columns), lambda k, s: (0, s[owner_at])),
                pl.BlockSpec((depth, columns), lambda k, s: (0, 0)),
                pl.BlockSpec((1, rows, columns), lambda k, s: (0, 0, 0)),
            ],
            out_specs=pl.BlockSpec((rows, columns), lambda k, s: (0, 0)),
        ),
        out_shape=jax.ShapeDtypeStruct((rows, columns), jnp.float32),
        compiler_params=pltpu.CompilerParams(vmem_limit_bytes=32 * MIB),
        cost_estimate=pl.CostEstimate(
            flops=2 * rows * columns * depth,
            bytes_accessed=2 * columns * (depth + rows * 4),
            transcendentals=0,
        ),
        name="sum_ahead",
    )(scalars, attended, tokens, shard, term)


def last_kernel(scalars, ahead, term, held, out):
    out[...] = (ahead[...] + term[0].astype(jnp.float32)).astype(jnp.bfloat16)


def last_rows(scalars, owner_at, ahead, term, held):
    rows, columns = ahead.shape
    return pl.pallas_call(
        last_kernel,
        grid_spec=pltpu.PrefetchScalarGridSpec(
            num_scalar_prefetch=1,
            grid=(1,),
            in_specs=[
                pl.BlockSpec((rows, columns), lambda k, s: (0, 0)),
                pl.BlockSpec((1, rows, columns), lambda k, s: (0, 0, 0)),
                pl.BlockSpec(memory_space=pl.ANY),
            ],
            out_specs=pl.BlockSpec((rows, columns), lambda k, s: (0, s[owner_at])),
        ),
        out_shape=jax.ShapeDtypeStruct(held.shape, held.dtype),
        input_output_aliases={3: 0},
        compiler_params=pltpu.CompilerParams(vmem_limit_bytes=32 * MIB),
        cost_estimate=pl.CostEstimate(
            flops=rows * columns, bytes_accessed=8 * rows * columns, transcendentals=0
        ),
        name="last_rows",
    )(scalars, ahead, term, held)


def add_rounded(a, b):
    return (a.astype(jnp.float32) + b.astype(jnp.float32)).astype(jnp.bfloat16)


def by_links(tokens, norm_gain, w_qkv, qk_gain, w_out, lengths):
    shard_rows, depth = tokens.shape
    n_windows = lengths.shape[1]
    width = w_qkv.shape[2]
    capacity = 4 * shard_rows
    weights = jnp.transpose(w_qkv, (1, 0, 2))
    gain = norm_gain.reshape(1, depth)
    head_gain = qk_gain.reshape(2, 1, width)
    owners_at = LENGTHS + n_windows

    def ring(array):
        return lax.ppermute(array, "dp", RING)

    def across_x(array):
        return lax.ppermute(array, "dp", ACROSS_X)

    def over_tensor(array, pairs):
        return lax.ppermute(array, "tensor", pairs)

    def far(index, rows, qkv, shards):
        return far_rows(
            scalars, index, n_windows, rows, gain, weights, head_gain, qkv, shards
        )

    def of_core(core):
        return core

    def of_other(core):
        return 1 - core

    together = lax.optimization_barrier

    far_a = over_tensor(tokens, over_y(0))
    r1, x0 = ring(w_out), across_x(w_out)
    other = over_tensor(tokens, ACROSS_CORE)
    tensor = lax.axis_index("tensor")
    table = jnp.asarray([arrivals(device) for device in range(8)], jnp.int32)
    scalars = jnp.concatenate(
        [jnp.stack([tensor % 2, tensor // 2]), lengths[0], table[lax.axis_index("dp")]]
    ).astype(jnp.int32)
    qkv = near_rows(scalars, tokens, other, gain, weights, head_gain, capacity)
    far_a, r1, x0, qkv, tokens_b, scalars = together((far_a, r1, x0, qkv, tokens, scalars))

    far_b = over_tensor(tokens_b, over_y(1))
    r2, x1 = ring(r1), across_x(r1)
    swap_a = over_tensor(far_a, from_core(0))
    qkv, attended_a, part_a1 = far(0, [far_a, swap_a], qkv, [w_out, r1, x0])
    sent_a1 = add_rounded(part_a1, over_tensor(part_a1, from_core(1)))
    far_b, r2, x1, qkv, attended_a, sent_a1 = together((far_b, r2, x1, qkv, attended_a, sent_a1))

    swap_b = over_tensor(far_b, from_core(1))
    (part_a2,) = out_rows(scalars, [attended_a], [r2, x1], [lambda core: 0])
    r3, x2 = ring(r2), across_x(r2)
    sum_a1 = over_tensor(sent_a1, over_y(0))
    sum_a2 = over_tensor(part_a2, ACROSS_Y)
    early = [w_out, r1, x0, r2, x1]
    qkv, attended_b, part_b = far(1, [swap_b, far_b], qkv, early)
    r3, x2, sum_a1, sum_a2, qkv, attended_b, part_b = together(
        (r3, x2, sum_a1, sum_a2, qkv, attended_b, part_b)
    )

    arrived_b = over_tensor(part_b, from_core(0))
    both = [of_core, of_other]
    mine_2, theirs_2 = out_rows(scalars, [attended_a, attended_b], [r3, x2], both)
    arrived_b, mine_2, theirs_2, r3, x2 = together((arrived_b, mine_2, theirs_2, r3, x2))

    sum_b = over_tensor(add_rounded(part_b, arrived_b), over_y(1))
    half = r3.shape[0] // 2
    x3_a, x3_b = across_x(r3[:half]), ring(x2[half:])
    arrived_2 = over_tensor(theirs_2, ACROSS_CORE)
    sum_a2_other = over_tensor(sum_a2, from_core(1))
    attended_near = attention_rows(scalars, n_windows, qkv, lambda s: s[Y] * 2, 2)
    (theirs_1,) = out_rows(scalars, [attended_near], [*early, r3, x2], [of_other])
    sent_2 = add_rounded(mine_2, arrived_2)
    x3 = jnp.concatenate([x3_a, x3_b], axis=0)
    sum_b, x3, sent_2, theirs_1, attended_near, sum_a2_other = together(
        (sum_b, x3, sent_2, theirs_1, attended_near, sum_a2_other)
    )

    def final(first, shards, terms, held):
        return final_rows(
            scalars, owners_at, first, attended_near, tokens, shards, terms, held
        )

    sum_2 = over_tensor(sent_2, ACROSS_Y)
    near_1 = over_tensor(theirs_1, ACROSS_CORE)
    mine_3, theirs_3, theirs_1 = out_rows(
        scalars,
        [attended_a, attended_b, attended_near],
        [x3],
        [of_core, of_other, lambda core: 3 - core],
    )
    arrived_3 = over_tensor(theirs_3, ACROSS_CORE)
    near_2 = over_tensor(theirs_1, ACROSS_CORE)
    out = final(0, early[:3], [(near_1, 0, None), (sum_a1, 0, 0), (sum_b, 0, 1)], None)
    terms = [(near_1, 3, None), (sum_a2, 0, 0), (sum_a2_other, 0, 0), (sum_b, 3, 1)]
    out = final(3, early[3:], terms, out)
    sum_2, arrived_3, near_2, mine_3, out = together((sum_2, arrived_3, near_2, mine_3, out))

    sum_3 = over_tensor(add_rounded(mine_3, arrived_3), ACROSS_Y)
    out = final(5, [r3, x2], [(near_1, 5, None), (sum_2, 0, None)], out)
    ahead = sum_ahead(scalars, owners_at + 7, attended_near, tokens, x3, near_2)
    return last_rows(scalars, owners_at + 7, ahead, sum_3, out)


def by_collectives(tokens, norm_gain, w_qkv, qk_gain, w_out, lengths):
    x_float = tokens.astype(jnp.float32)
    normed = (unit_rms(x_float, EPS_ROW) * norm_gain).astype(jnp.bfloat16)
    gathered = lax.all_gather(normed, "tensor", axis=0, tiled=True)
    full_out = lax.all_gather(w_out, "dp", axis=1, tiled=True)
    capacity = gathered.shape[0]
    _, heads, head_size = qk_gain.shape
    local_width = w_qkv.shape[2]
    qkv = jnp.dot(
        gathered, w_qkv.reshape(w_qkv.shape[0], 3 * local_width), preferred_element_type=jnp.float32
    ).reshape(capacity, 3, heads, head_size)
    queries = (unit_rms(qkv[:, 0], EPS_HEAD) * qk_gain[0]).astype(jnp.bfloat16)
    keys = (unit_rms(qkv[:, 1], EPS_HEAD) * qk_gain[1]).astype(jnp.bfloat16)
    values = qkv[:, 2].astype(jnp.bfloat16)
    ends = jnp.cumsum(lengths[0])
    places = jnp.arange(capacity, dtype=jnp.int32)
    segment = jnp.sum((places[:, None] >= ends[None, :]).astype(jnp.int32), axis=1)
    seen = (segment[:, None] == segment[None, :]) & (places[None, :] <= places[:, None])
    scores = jnp.einsum("qhd,khd->hqk", queries, keys, preferred_element_type=jnp.float32)
    scores = jnp.where(seen[None], scores * head_size ** (-0.5), -jnp.inf)
    expo = jnp.exp(scores - jnp.max(scores, axis=2, keepdims=True))
    total = jnp.sum(expo, axis=2, keepdims=True)
    summed = jnp.einsum(
        "hqk,khd->qhd", expo.astype(jnp.bfloat16), values, preferred_element_type=jnp.float32
    )
    attended = (summed / jnp.transpose(total, (1, 0, 2))).astype(jnp.bfloat16)
    partial = jnp.dot(
        attended.reshape(capacity, local_width), full_out, preferred_element_type=jnp.float32
    ).astype(jnp.bfloat16)
    reduced = lax.psum_scatter(partial, "tensor", scatter_dimension=0, tiled=True)
    return (x_float + reduced.astype(jnp.float32)).astype(jnp.bfloat16)


def solution(mesh):
    placed = (
        P(("dp", "tensor"), None),
        P(),
        P(None, None, "tensor"),
        P(None, "tensor", None),
        P("tensor", "dp"),
        P("dp", None),
    )
    known = mesh.shape["dp"] == 8 and mesh.shape["tensor"] == 4
    return jax.shard_map(
        by_links if known else by_collectives,
        mesh=mesh,
        in_specs=placed,
        out_specs=P(("dp", "tensor"), None),
        check_vma=False,
    )
```

```python
import math

import jax
import jax.numpy as jnp
from jax import lax
from jax.experimental import pallas as pl
from jax.experimental.pallas import tpu as pltpu
from jax.sharding import PartitionSpec as P

EPS_ROW = 1e-05
EPS_HEAD = 1e-06
MIB = 1024 * 1024
BLOCK = 256
HEAD = 128
CORE, Y, LENGTHS = 0, 1, 2


def unit_rms(values, epsilon):
    return values * lax.rsqrt(jnp.mean(values * values, axis=-1, keepdims=True) + epsilon)


SLOTS = 3


def weight_copies(weights, columns, held, sems):
    per = weights.shape[2] // columns

    def copy(step):
        at = pl.multiple_of(step % per * columns, columns)
        block = weights.at[step // per, :, pl.ds(at, columns)]
        return pltpu.make_async_copy(block, held.at[step % SLOTS], sems.at[step % SLOTS])

    return copy


def project(step, per, normed, copy, held, products, head_gain, out):
    def finish(product):
        which = (step - 1) // per
        for head in range(product.shape[1] // HEAD):
            lanes = slice(head * HEAD, (head + 1) * HEAD)
            value = product[:, lanes]
            one = unit_rms(value, EPS_HEAD) * head_gain[0, :, lanes]
            out[0, :, lanes] = jnp.where(which < 2, one, value).astype(jnp.bfloat16)

    @pl.when((step >= 1) & (step + SLOTS - 1 < 3 * per))
    def _():
        copy(step + SLOTS - 1).start()

    for parity in range(2):

        @pl.when((step < 3 * per) & (step % 2 == parity))
        def _(parity=parity):
            copy(step).wait()
            finish(products[1 - parity])
            products[parity][...] = jnp.dot(
                normed[...], held[step % SLOTS], preferred_element_type=jnp.float32
            )

    @pl.when(step == 3 * per)
    def _():
        finish(products[(3 * per - 1) % 2])


def near_kernel(scalars, own, other, gain, weights, head_gain, out, normed, held, sems, *products):
    step = pl.program_id(0)
    copy = weight_copies(weights, out.shape[2], held, sems)

    @pl.when(step == 0)
    def _():
        for number in range(SLOTS):
            copy(number).start()
        size = 64
        for piece, core in ((own, scalars[CORE]), (other, 1 - scalars[CORE])):

            def rows(number, carry, piece=piece, core=core):
                first = pl.multiple_of(number * size, size)
                one = piece[pl.ds(first, size), :].astype(jnp.float32)
                one = unit_rms(one, EPS_ROW) * gain[...]
                to = pl.multiple_of(core * piece.shape[0] + first, size)
                normed[pl.ds(to, size), :] = one.astype(jnp.bfloat16)
                return carry

            lax.fori_loop(0, piece.shape[0] // size, rows, 0)

    project(
        step, weights.shape[2] // out.shape[2], normed, copy, held, products, head_gain, out
    )


def finished(per):
    def at(step):
        block = jnp.clip(step - 1, 0, 3 * per - 1)
        return block // per, block % per

    return at


def near_rows(scalars, own, other, gain, weights, head_gain, capacity):
    depth, width = weights.shape[1], weights.shape[2]
    rows = own.shape[0] + other.shape[0]
    block = min(2 * BLOCK, width)
    per = width // block
    at = finished(per)
    once = pl.Buffered(1)
    return pl.pallas_call(
        near_kernel,
        grid_spec=pltpu.PrefetchScalarGridSpec(
            num_scalar_prefetch=1,
            grid=(3 * per + 1,),
            in_specs=[
                pl.BlockSpec(own.shape, lambda i, s: (0, 0), pipeline_mode=once),
                pl.BlockSpec(other.shape, lambda i, s: (0, 0), pipeline_mode=once),
                pl.BlockSpec((1, depth), lambda i, s: (0, 0)),
                pl.BlockSpec(memory_space=pl.ANY),
                pl.BlockSpec((1, 1, block), lambda i, s: (jnp.minimum(at(i)[0], 1), 0, at(i)[1])),
            ],
            out_specs=pl.BlockSpec((1, rows, block), lambda i, s: (at(i)[0], s[Y], at(i)[1])),
            scratch_shapes=[
                pltpu.VMEM((rows, depth), jnp.bfloat16),
                pltpu.VMEM((SLOTS, depth, block), jnp.bfloat16),
                pltpu.SemaphoreType.DMA((SLOTS,)),
                pltpu.VMEM((rows, block), jnp.float32),
                pltpu.VMEM((rows, block), jnp.float32),
            ],
        ),
        out_shape=jax.ShapeDtypeStruct((3, capacity, width), jnp.bfloat16),
        compiler_params=pltpu.CompilerParams(vmem_limit_bytes=48 * MIB),
        cost_estimate=pl.CostEstimate(
            flops=2 * rows * depth * 3 * width,
            bytes_accessed=2 * (3 * depth * width + rows * depth + 3 * rows * width),
            transcendentals=0,
        ),
        name="near_rows",
    )(scalars, own, other, gain, weights, head_gain)


def attend_block(scalars, n_windows, at, queries, rows_of, hidden, out):
    block, width = out.shape
    first = at * block
    ends = []
    running = jnp.int32(0)
    for index in range(n_windows):
        running = running + scalars[LENGTHS + index]
        ends.append(running)
    opens = jnp.int32(0)
    for end in ends:
        opens = jnp.where(first >= end, end, opens)
    count = at - opens // block + 1
    factor = HEAD ** (-0.5) * math.log2(math.e)

    def attend(blocks):
        span = blocks * block
        start = (at - blocks + 1) * block
        row = first + lax.broadcasted_iota(jnp.int32, (block, 1), 0)
        window = jnp.zeros_like(row)
        for end in ends:
            window = jnp.where(row >= end, end, window)
        column = start + lax.broadcasted_iota(jnp.int32, (block, span), 1)
        hidden[:, :span] = jnp.where((column <= row) & (column >= window), 0.0, -jnp.inf)
        keys, values, place = rows_of(blocks)
        for head in range(width // HEAD):
            lanes = slice(head * HEAD, (head + 1) * HEAD)
            scores = lax.dot_general(
                queries[:, lanes],
                keys[pl.ds(place, span), lanes],
                (((1,), (1,)), ((), ())),
                preferred_element_type=jnp.float32,
            )
            scores = scores + hidden[:, :span]
            top = jnp.max(scores, axis=1, keepdims=True)
            expo = jnp.exp2((scores - top) * factor)
            total = jnp.sum(expo, axis=1, keepdims=True)
            summed = jnp.dot(
                expo.astype(jnp.bfloat16),
                values[pl.ds(place, span), lanes],
                preferred_element_type=jnp.float32,
            )
            out[:, lanes] = (summed / total).astype(jnp.bfloat16)

    for blocks in (1, 2, 3):
        pl.when(count == blocks)(lambda blocks=blocks: attend(blocks))


def attention_kernel(first_block, n_windows, scalars, queries, keys, values, out, hidden):
    at = first_block(scalars) + pl.program_id(0)

    def rows_of(blocks):
        return keys.at[0], values.at[0], pl.multiple_of((at - blocks + 1) * BLOCK, BLOCK)

    attend_block(scalars, n_windows, at, queries.at[0], rows_of, hidden, out)


def attention_rows(scalars, n_windows, qkv, first_block, n_blocks):
    _, capacity, width = qkv.shape
    return pl.pallas_call(
        lambda *refs: attention_kernel(first_block, n_windows, *refs),
        grid_spec=pltpu.PrefetchScalarGridSpec(
            num_scalar_prefetch=1,
            grid=(n_blocks,),
            in_specs=[
                pl.BlockSpec((1, BLOCK, width), lambda b, s: (0, first_block(s) + b, 0)),
                pl.BlockSpec((1, capacity, width), lambda b, s: (1, 0, 0)),
                pl.BlockSpec((1, capacity, width), lambda b, s: (2, 0, 0)),
            ],
            out_specs=pl.BlockSpec((BLOCK, width), lambda b, s: (b, 0)),
            scratch_shapes=[pltpu.VMEM((BLOCK, 3 * BLOCK), jnp.float32)],
        ),
        out_shape=jax.ShapeDtypeStruct((n_blocks * BLOCK, width), jnp.bfloat16),
        compiler_params=pltpu.CompilerParams(vmem_limit_bytes=32 * MIB),
        cost_estimate=pl.CostEstimate(
            flops=4 * n_blocks * BLOCK * 3 * BLOCK * width,
            bytes_accessed=2 * (2 * capacity * width + 2 * n_blocks * BLOCK * width),
            transcendentals=n_blocks * BLOCK * 3 * BLOCK * width // HEAD,
        ),
        name="attention_rows",
    )(scalars, qkv, qkv, qkv)


def far_kernel(index, n_windows, n_shards, scalars, core0_rows, core1_rows, gain, weights, head_gain, *refs):
    qkv_held, shards = refs[0], refs[1 : 1 + n_shards]
    out_qkv, out_attended, out_partial = refs[1 + n_shards : 4 + n_shards]
    normed, queries, keys, values, hidden, held, sems, blocks, block_sems, ready, sent = refs[
        4 + n_shards : 15 + n_shards
    ]
    products = refs[15 + n_shards :]
    step = pl.program_id(0)
    block, width = out_attended.shape
    columns = out_qkv.shape[2]
    per = width // columns
    at = (1 - scalars[Y]) * 2 + index
    block_copy = weight_copies(weights, columns, blocks, block_sems)
    copies = [
        pltpu.make_async_copy(shard, held.at[number], sems.at[number])
        for number, shard in enumerate(shards)
    ]

    def leaves(number):
        return pltpu.make_async_copy(ready.at[number], out_partial.at[number], sent.at[number])

    def older(back, which, to):
        rows = qkv_held.at[which, pl.ds(pl.multiple_of((at - back) * block, block), block)]
        place = to.at[(2 - back) * block : (3 - back) * block]
        return pltpu.make_async_copy(rows, place, sems.at[n_shards + 2 * back + which - 3])

    def all_older(do):
        for back in (1, 2):

            @pl.when(at >= back)
            def _(back=back):
                do(older(back, 1, keys))
                do(older(back, 2, values))

    @pl.when(step == 0)
    def _():
        for number in range(SLOTS):
            block_copy(number).start()
        all_older(lambda copy: copy.start())
        for copy in copies:
            copy.start()
        size = 64

        def rows(number, carry):
            first = pl.multiple_of(number * size, size)
            one = core0_rows[pl.ds(first, size), :].astype(jnp.float32)
            other = core1_rows[pl.ds(first, size), :].astype(jnp.float32)
            one = unit_rms(jnp.where(scalars[CORE] == 0, one, other), EPS_ROW) * gain[...]
            normed[pl.ds(first, size), :] = one.astype(jnp.bfloat16)
            return carry

        lax.fori_loop(0, block // size, rows, 0)

    project(step, per, normed, block_copy, blocks, products, head_gain, out_qkv)

    for number in range(3 * per):
        lanes = slice(number % per * columns, (number % per + 1) * columns)
        to = (queries, keys, values)[number // per]
        first = 0 if number < per else 2 * block

        @pl.when(step == number + 1)
        def _(to=to, lanes=lanes, first=first):
            to[first : first + block, lanes] = out_qkv[0]

    @pl.when(step == 3 * per)
    def _():
        all_older(lambda copy: copy.wait())
        attend_block(
            scalars, n_windows, at, queries, lambda blocks: (keys, values, (3 - blocks) * block), hidden, out_attended
        )
        for number, copy in enumerate(copies):
            copy.wait()
            product = jnp.dot(out_attended[...], held[number], preferred_element_type=jnp.float32)
            ready[number] = product.astype(jnp.bfloat16)
            leaves(number).start()
        for number in range(n_shards):
            leaves(number).wait()


def far_rows(scalars, index, n_windows, rows, gain, weights, head_gain, qkv, shards):
    block, depth = rows[0].shape
    _, capacity, width = qkv.shape
    columns = min(2 * BLOCK, width)
    per = width // columns
    n = len(shards)
    shard_shape = shards[0].shape
    at = finished(per)
    once = pl.Buffered(1)
    whole = [pl.BlockSpec((block, depth), lambda i, s: (0, 0), pipeline_mode=once)] * 2
    somewhere = pl.BlockSpec(memory_space=pl.ANY)
    return pl.pallas_call(
        lambda *refs: far_kernel(index, n_windows, n, *refs),
        grid_spec=pltpu.PrefetchScalarGridSpec(
            num_scalar_prefetch=1,
            grid=(3 * per + 1,),
            in_specs=[
                *whole,
                pl.BlockSpec((1, depth), lambda i, s: (0, 0)),
                somewhere,
                pl.BlockSpec((1, 1, columns), lambda i, s: (jnp.minimum(at(i)[0], 1), 0, at(i)[1])),
                *[somewhere] * (1 + n),
            ],
            out_specs=[
                pl.BlockSpec(
                    (1, block, columns),
                    lambda i, s: (at(i)[0], (1 - s[Y]) * 2 + index, at(i)[1]),
                ),
                pl.BlockSpec((block, width), lambda i, s: (0, 0)),
                somewhere,
            ],
            scratch_shapes=[
                pltpu.VMEM((block, depth), jnp.bfloat16),
                pltpu.VMEM((block, width), jnp.bfloat16),
                pltpu.VMEM((3 * block, width), jnp.bfloat16),
                pltpu.VMEM((3 * block, width), jnp.bfloat16),
                pltpu.VMEM((block, 3 * block), jnp.float32),
                pltpu.VMEM((n, *shard_shape), jnp.bfloat16),
                pltpu.SemaphoreType.DMA((n + 4,)),
                pltpu.VMEM((SLOTS, depth, columns), jnp.bfloat16),
                pltpu.SemaphoreType.DMA((SLOTS,)),
                pltpu.VMEM((n, block, shard_shape[1]), jnp.bfloat16),
                pltpu.SemaphoreType.DMA((n,)),
                pltpu.VMEM((block, columns), jnp.float32),
                pltpu.VMEM((block, columns), jnp.float32),
            ],
        ),
        out_shape=[
            jax.ShapeDtypeStruct(qkv.shape, jnp.bfloat16),
            jax.ShapeDtypeStruct((block, width), jnp.bfloat16),
            jax.ShapeDtypeStruct((n, block, shard_shape[1]), jnp.bfloat16),
        ],
        input_output_aliases={6: 0},
        compiler_params=pltpu.CompilerParams(vmem_limit_bytes=56 * MIB),
        cost_estimate=pl.CostEstimate(
            flops=2 * block * width * (3 * depth + 6 * block + n * shard_shape[1]),
            bytes_accessed=2 * (3 * depth * width + 2 * block * depth + n * shard_shape[1] * width),
            transcendentals=block * 3 * block * width // HEAD,
        ),
        name="far_rows",
    )(scalars, *rows, gain, weights, head_gain, qkv, *shards)


def out_kernel(n_inputs, n_shards, wanted, scalars, *refs):
    inputs, shards = refs[:n_inputs], refs[n_inputs : n_inputs + n_shards]
    outs = refs[n_inputs + n_shards : -4]
    rows_held, rows_arrived, held, arrived = refs[-4:]
    copies, at = [], 0
    for index, part in enumerate(inputs):
        to = rows_held.at[at : at + part.shape[0]]
        copies.append(pltpu.make_async_copy(part, to, rows_arrived.at[index]))
        at += part.shape[0]
    shard_copies = [
        pltpu.make_async_copy(shard, held.at[index], arrived.at[index])
        for index, shard in enumerate(shards)
    ]
    for copy in copies + shard_copies:
        copy.start()
    for copy in copies:
        copy.wait()
    rows = outs[0].shape[1]
    for index, copy in enumerate(shard_copies):
        copy.wait()
        for out, which in zip(outs, wanted, strict=True):
            place = pl.multiple_of(which(scalars[CORE]) * rows, rows)
            product = jnp.dot(
                rows_held[pl.ds(place, rows), :], held[index], preferred_element_type=jnp.float32
            )
            out[index] = product.astype(jnp.bfloat16)


def out_rows(scalars, inputs, shards, wanted):
    total = sum(part.shape[0] for part in inputs)
    depth, columns = shards[0].shape
    n, n_inputs, n_outs = len(shards), len(inputs), len(wanted)
    shape = jax.ShapeDtypeStruct((n, BLOCK, columns), jnp.bfloat16)
    whole = pl.BlockSpec(memory_space=pltpu.VMEM)
    return pl.pallas_call(
        lambda *refs: out_kernel(n_inputs, n, wanted, *refs),
        in_specs=[pl.BlockSpec(memory_space=pltpu.SMEM)]
        + [pl.BlockSpec(memory_space=pl.ANY)] * (n_inputs + n),
        out_specs=[whole] * n_outs,
        out_shape=[shape] * n_outs,
        scratch_shapes=[
            pltpu.VMEM((total, depth), jnp.bfloat16),
            pltpu.SemaphoreType.DMA((n_inputs,)),
            pltpu.VMEM((n, depth, columns), jnp.bfloat16),
            pltpu.SemaphoreType.DMA((n,)),
        ],
        compiler_params=pltpu.CompilerParams(vmem_limit_bytes=32 * MIB),
        cost_estimate=pl.CostEstimate(
            flops=2 * n_outs * BLOCK * depth * columns * n,
            bytes_accessed=2 * (total * depth + n * columns * (depth + n_outs * BLOCK)),
            transcendentals=0,
        ),
        name="out_rows",
    )(scalars, *inputs, *shards)


def final_kernel(n, cores, scalars, attended, tokens, *refs):
    terms, shards = refs[: len(cores)], refs[len(cores) : len(cores) + n]
    out, held, arrived = refs[-3:]
    step = pl.program_id(0)
    copies = [
        pltpu.make_async_copy(shard, held.at[index], arrived.at[index])
        for index, shard in enumerate(shards)
    ]

    @pl.when(step == 0)
    def _():
        for copy in copies:
            copy.start()

    for index, copy in enumerate(copies):
        pl.when(step == index)(copy.wait)
    product = jnp.dot(attended[...], held[step], preferred_element_type=jnp.float32)
    summed = product.astype(jnp.bfloat16).astype(jnp.float32)
    for term, core in zip(terms, cores, strict=True):
        value = term[0].astype(jnp.float32)
        if core is not None:
            value = jnp.where(scalars[CORE] == core, value, 0.0)
        summed = summed + value
    out[...] = (tokens[...].astype(jnp.float32) + summed).astype(jnp.bfloat16)


def final_rows(scalars, owners_at, first, attended, tokens, shards, terms, held):
    n = len(shards)
    rows = tokens.shape[0]
    depth, columns = shards[0].shape
    placed = pl.BlockSpec((rows, columns), lambda k, s: (0, s[owners_at + first + k]))
    in_specs = [pl.BlockSpec((rows, depth), lambda k, s: (s[CORE], 0)), placed]
    operands = [scalars, attended, tokens]
    for array, offset, _ in terms:
        in_specs.append(
            pl.BlockSpec((1, rows, columns), lambda k, s, offset=offset: (k + offset, 0, 0))
        )
        operands.append(array)
    in_specs += [pl.BlockSpec(memory_space=pl.ANY)] * n
    operands += shards
    aliases = {}
    if held is not None:
        in_specs.append(pl.BlockSpec(memory_space=pl.ANY))
        operands.append(held)
        aliases = {len(operands) - 1: 0}
    cores = [core for _, _, core in terms]
    return pl.pallas_call(
        lambda *refs: final_kernel(n, cores, *refs),
        grid_spec=pltpu.PrefetchScalarGridSpec(
            num_scalar_prefetch=1,
            grid=(n,),
            in_specs=in_specs,
            out_specs=placed,
            scratch_shapes=[
                pltpu.VMEM((n, depth, columns), jnp.bfloat16),
                pltpu.SemaphoreType.DMA((n,)),
            ],
        ),
        out_shape=jax.ShapeDtypeStruct(tokens.shape, jnp.bfloat16),
        input_output_aliases=aliases,
        compiler_params=pltpu.CompilerParams(vmem_limit_bytes=32 * MIB),
        cost_estimate=pl.CostEstimate(
            flops=2 * n * rows * columns * depth,
            bytes_accessed=2 * n * columns * (depth + rows * (2 + len(terms))),
            transcendentals=0,
        ),
        name="final_rows",
    )(*operands)


NEXT_Z = {0: 1, 1: 3, 3: 2, 2: 0}
BACK_Z = {after: before for before, after in NEXT_Z.items()}
RING = [(2 * z + x, 2 * NEXT_Z[z] + x) for z in range(4) for x in range(2)]
ACROSS_X = [(d, d ^ 1) for d in range(8)]
ACROSS_CORE = [(t, t ^ 1) for t in range(4)]
ACROSS_Y = [(t, t ^ 2) for t in range(4)]


def arrivals(device):
    z, x = [device // 2], device % 2
    for _ in range(3):
        z.append(BACK_Z[z[-1]])
    held_by = [(0, x), (1, x), (0, 1 - x), (2, x), (1, 1 - x), (3, x), (2, 1 - x), (3, 1 - x)]
    return [2 * z[steps] + from_x for steps, from_x in held_by]


def from_core(core):
    return [(t, t ^ 1) for t in range(4) if t % 2 == core]


def over_y(core):
    return [(t, t ^ 2) for t in range(4) if t % 2 == core]


def ahead_kernel(scalars, attended, tokens, shard, term, out):
    product = jnp.dot(attended[...], shard[...], preferred_element_type=jnp.float32)
    summed = product.astype(jnp.bfloat16).astype(jnp.float32) + term[0].astype(jnp.float32)
    out[...] = tokens[...].astype(jnp.float32) + summed


def sum_ahead(scalars, owner_at, attended, tokens, shard, term):
    rows = tokens.shape[0]
    depth, columns = shard.shape
    return pl.pallas_call(
        ahead_kernel,
        grid_spec=pltpu.PrefetchScalarGridSpec(
            num_scalar_prefetch=1,
            grid=(1,),
            in_specs=[
                pl.BlockSpec((rows, depth), lambda k, s: (s[CORE], 0)),
                pl.BlockSpec((rows, columns), lambda k, s: (0, s[owner_at])),
                pl.BlockSpec((depth, columns), lambda k, s: (0, 0)),
                pl.BlockSpec((1, rows, columns), lambda k, s: (0, 0, 0)),
            ],
            out_specs=pl.BlockSpec((rows, columns), lambda k, s: (0, 0)),
        ),
        out_shape=jax.ShapeDtypeStruct((rows, columns), jnp.float32),
        compiler_params=pltpu.CompilerParams(vmem_limit_bytes=32 * MIB),
        cost_estimate=pl.CostEstimate(
            flops=2 * rows * columns * depth,
            bytes_accessed=2 * columns * (depth + rows * 4),
            transcendentals=0,
        ),
        name="sum_ahead",
    )(scalars, attended, tokens, shard, term)


def last_kernel(scalars, ahead, term, held, out):
    out[...] = (ahead[...] + term[0].astype(jnp.float32)).astype(jnp.bfloat16)


def last_rows(scalars, owner_at, ahead, term, held):
    rows, columns = ahead.shape
    return pl.pallas_call(
        last_kernel,
        grid_spec=pltpu.PrefetchScalarGridSpec(
            num_scalar_prefetch=1,
            grid=(1,),
            in_specs=[
                pl.BlockSpec((rows, columns), lambda k, s: (0, 0)),
                pl.BlockSpec((1, rows, columns), lambda k, s: (0, 0, 0)),
                pl.BlockSpec(memory_space=pl.ANY),
            ],
            out_specs=pl.BlockSpec((rows, columns), lambda k, s: (0, s[owner_at])),
        ),
        out_shape=jax.ShapeDtypeStruct(held.shape, held.dtype),
        input_output_aliases={3: 0},
        compiler_params=pltpu.CompilerParams(vmem_limit_bytes=32 * MIB),
        cost_estimate=pl.CostEstimate(
            flops=rows * columns, bytes_accessed=8 * rows * columns, transcendentals=0
        ),
        name="last_rows",
    )(scalars, ahead, term, held)


def add_rounded(a, b):
    return (a.astype(jnp.float32) + b.astype(jnp.float32)).astype(jnp.bfloat16)


def by_links(tokens, norm_gain, w_qkv, qk_gain, w_out, lengths):
    shard_rows, depth = tokens.shape
    n_windows = lengths.shape[1]
    width = w_qkv.shape[2]
    capacity = 4 * shard_rows
    weights = jnp.transpose(w_qkv, (1, 0, 2))
    gain = norm_gain.reshape(1, depth)
    head_gain = qk_gain.reshape(2, 1, width)
    owners_at = LENGTHS + n_windows

    def ring(array):
        return lax.ppermute(array, "dp", RING)

    def across_x(array):
        return lax.ppermute(array, "dp", ACROSS_X)

    def over_tensor(array, pairs):
        return lax.ppermute(array, "tensor", pairs)

    def far(index, rows, qkv, shards):
        return far_rows(
            scalars, index, n_windows, rows, gain, weights, head_gain, qkv, shards
        )

    def of_core(core):
        return core

    def of_other(core):
        return 1 - core

    together = lax.optimization_barrier

    far_a = over_tensor(tokens, over_y(0))
    r1, x0 = ring(w_out), across_x(w_out)
    other = over_tensor(tokens, ACROSS_CORE)
    tensor = lax.axis_index("tensor")
    table = jnp.asarray([arrivals(device) for device in range(8)], jnp.int32)
    scalars = jnp.concatenate(
        [jnp.stack([tensor % 2, tensor // 2]), lengths[0], table[lax.axis_index("dp")]]
    ).astype(jnp.int32)
    qkv = near_rows(scalars, tokens, other, gain, weights, head_gain, capacity)
    far_a, r1, x0, qkv, tokens_b, scalars = together((far_a, r1, x0, qkv, tokens, scalars))

    far_b = over_tensor(tokens_b, over_y(1))
    r2, x1 = ring(r1), across_x(r1)
    swap_a = over_tensor(far_a, from_core(0))
    qkv, attended_a, part_a1 = far(0, [far_a, swap_a], qkv, [w_out, r1, x0])
    sent_a1 = add_rounded(part_a1, over_tensor(part_a1, from_core(1)))
    far_b, r2, x1, qkv, attended_a, sent_a1 = together((far_b, r2, x1, qkv, attended_a, sent_a1))

    swap_b = over_tensor(far_b, from_core(1))
    (part_a2,) = out_rows(scalars, [attended_a], [r2, x1], [lambda core: 0])
    r3, x2 = ring(r2), across_x(r2)
    sum_a1 = over_tensor(sent_a1, over_y(0))
    sum_a2 = over_tensor(part_a2, ACROSS_Y)
    early = [w_out, r1, x0, r2, x1]
    qkv, attended_b, part_b = far(1, [swap_b, far_b], qkv, early)
    r3, x2, sum_a1, sum_a2, qkv, attended_b, part_b = together(
        (r3, x2, sum_a1, sum_a2, qkv, attended_b, part_b)
    )

    arrived_b = over_tensor(part_b, from_core(0))
    both = [of_core, of_other]
    mine_2, theirs_2 = out_rows(scalars, [attended_a, attended_b], [r3, x2], both)
    arrived_b, mine_2, theirs_2, r3, x2 = together((arrived_b, mine_2, theirs_2, r3, x2))

    sum_b = over_tensor(add_rounded(part_b, arrived_b), over_y(1))
    half = r3.shape[0] // 2
    x3_a, x3_b = across_x(r3[:half]), ring(x2[half:])
    arrived_2 = over_tensor(theirs_2, ACROSS_CORE)
    sum_a2_other = over_tensor(sum_a2, from_core(1))
    attended_near = attention_rows(scalars, n_windows, qkv, lambda s: s[Y] * 2, 2)
    (theirs_1,) = out_rows(scalars, [attended_near], [*early, r3, x2], [of_other])
    sent_2 = add_rounded(mine_2, arrived_2)
    x3 = jnp.concatenate([x3_a, x3_b], axis=0)
    sum_b, x3, sent_2, theirs_1, attended_near, sum_a2_other = together(
        (sum_b, x3, sent_2, theirs_1, attended_near, sum_a2_other)
    )

    def final(first, shards, terms, held):
        return final_rows(
            scalars, owners_at, first, attended_near, tokens, shards, terms, held
        )

    sum_2 = over_tensor(sent_2, ACROSS_Y)
    near_1 = over_tensor(theirs_1, ACROSS_CORE)
    mine_3, theirs_3, theirs_1 = out_rows(
        scalars,
        [attended_a, attended_b, attended_near],
        [x3],
        [of_core, of_other, lambda core: 3 - core],
    )
    arrived_3 = over_tensor(theirs_3, ACROSS_CORE)
    near_2 = over_tensor(theirs_1, ACROSS_CORE)
    out = final(0, early[:3], [(near_1, 0, None), (sum_a1, 0, 0), (sum_b, 0, 1)], None)
    terms = [(near_1, 3, None), (sum_a2, 0, 0), (sum_a2_other, 0, 0), (sum_b, 3, 1)]
    out = final(3, early[3:], terms, out)
    sum_2, arrived_3, near_2, mine_3, out = together((sum_2, arrived_3, near_2, mine_3, out))

    sum_3 = over_tensor(add_rounded(mine_3, arrived_3), ACROSS_Y)
    out = final(5, [r3, x2], [(near_1, 5, None), (sum_2, 0, None)], out)
    ahead = sum_ahead(scalars, owners_at + 7, attended_near, tokens, x3, near_2)
    return last_rows(scalars, owners_at + 7, ahead, sum_3, out)


def by_collectives(tokens, norm_gain, w_qkv, qk_gain, w_out, lengths):
    x_float = tokens.astype(jnp.float32)
    normed = (unit_rms(x_float, EPS_ROW) * norm_gain).astype(jnp.bfloat16)
    gathered = lax.all_gather(normed, "tensor", axis=0, tiled=True)
    full_out = lax.all_gather(w_out, "dp", axis=1, tiled=True)
    capacity = gathered.shape[0]
    _, heads, head_size = qk_gain.shape
    local_width = w_qkv.shape[2]
    qkv = jnp.dot(
        gathered, w_qkv.reshape(w_qkv.shape[0], 3 * local_width), preferred_element_type=jnp.float32
    ).reshape(capacity, 3, heads, head_size)
    queries = (unit_rms(qkv[:, 0], EPS_HEAD) * qk_gain[0]).astype(jnp.bfloat16)
    keys = (unit_rms(qkv[:, 1], EPS_HEAD) * qk_gain[1]).astype(jnp.bfloat16)
    values = qkv[:, 2].astype(jnp.bfloat16)
    ends = jnp.cumsum(lengths[0])
    places = jnp.arange(capacity, dtype=jnp.int32)
    segment = jnp.sum((places[:, None] >= ends[None, :]).astype(jnp.int32), axis=1)
    seen = (segment[:, None] == segment[None, :]) & (places[None, :] <= places[:, None])
    scores = jnp.einsum("qhd,khd->hqk", queries, keys, preferred_element_type=jnp.float32)
    scores = jnp.where(seen[None], scores * head_size ** (-0.5), -jnp.inf)
    expo = jnp.exp(scores - jnp.max(scores, axis=2, keepdims=True))
    total = jnp.sum(expo, axis=2, keepdims=True)
    summed = jnp.einsum(
        "hqk,khd->qhd", expo.astype(jnp.bfloat16), values, preferred_element_type=jnp.float32
    )
    attended = (summed / jnp.transpose(total, (1, 0, 2))).astype(jnp.bfloat16)
    partial = jnp.dot(
        attended.reshape(capacity, local_width), full_out, preferred_element_type=jnp.float32
    ).astype(jnp.bfloat16)
    reduced = lax.psum_scatter(partial, "tensor", scatter_dimension=0, tiled=True)
    return (x_float + reduced.astype(jnp.float32)).astype(jnp.bfloat16)


def solution(mesh):
    placed = (
        P(("dp", "tensor"), None),
        P(),
        P(None, None, "tensor"),
        P(None, "tensor", None),
        P("tensor", "dp"),
        P("dp", None),
    )
    known = mesh.shape["dp"] == 8 and mesh.shape["tensor"] == 4
    return jax.shard_map(
        by_links if known else by_collectives,
        mesh=mesh,
        in_specs=placed,
        out_specs=P(("dp", "tensor"), None),
        check_vma=False,
    )
```
